256 devices in a mesh: feat: 8 (over z), clus: 32 (over y, x, core).
Axes of the slice: x: 4, y: 4, z: 8, core: 2. Of those that a mesh axis runs over, the one named last changes fastest.
Arguments:
- embeddings: bfloat16 [196608, 2048], P('clus', 'feat')
- signs: int32 [2048], P('feat'), may hold values from 0 to 1
- coords: int32 [512], replicated, may hold values from 0 to 2047, as said below
- cluster: int32 [196608], P('clus'), may hold values from 0 to 4095, as said below
- order: int32 [196608], P('clus'), may hold values from 0 to 196607, each once
Outputs:
- best: float32 [32, 6144], P('clus', 'feat')
The draws below stay inside these ranges and needn't reach their ends.
Inputs may be any that keep to these rules, and one draw needn't show every extreme that they name: Clusters belong to owners: cluster c belongs to owner c // 16. Among the 768 rows of each aligned block (rows of one device) at most 12 belong to one owner's clusters, and one owner receives exactly 12 rows from every block. `coords`: the sampled coordinates are distinct.
All inputs are finite; a program needn't handle non-finite values.
Results may differ from the reference program's by a relative error of at most 0.00035.
Values may be sent and summed in bfloat16 or wider, within the bound.
A program may use at most 128 MiB of HBM per device.

```python
import math
import jax
import jax.numpy as jnp
from jax import lax

EMB = 1280
DP = 2048
KEEP = 512
ROW_DEV = 768
CL_OWN = 16
OWNERS = 256
CAP = 12
ROWS = 196608
CLUSTERS = 4096
N_FEAT = 8
N_CLUS = 32


def routing(key):
    key = jax.random.fold_in(key, 11)
    key_hot, key_slots, key_shuffle, key_first, key_second = jax.random.split(key, 5)
    hot = jax.random.randint(key_hot, (), 0, OWNERS)
    slots = jnp.arange(OWNERS * CAP, dtype=jnp.int32)
    ranks = jax.vmap(lambda k: jax.random.permutation(k, OWNERS * CAP))(jax.random.split(key_slots, OWNERS)).astype(jnp.int32)
    scores = jnp.where((slots // CAP == hot)[None, :], slots[None, :] - OWNERS * CAP, ranks)
    chosen = jnp.argsort(scores, axis=1, stable=True)[:, :ROW_DEV].astype(jnp.int32)
    shuffle = jax.vmap(lambda k: jax.random.permutation(k, ROW_DEV))(jax.random.split(key_shuffle, OWNERS)).astype(jnp.int32)
    chosen = jnp.take_along_axis(chosen, shuffle, axis=1)
    owner = chosen // CAP
    first = jax.random.randint(key_first, (OWNERS, ROW_DEV), 0, CL_OWN)
    second = jax.random.randint(key_second, (OWNERS, ROW_DEV), 0, CL_OWN)
    return (owner * CL_OWN + jnp.minimum(first, second)).reshape(ROWS).astype(jnp.int32)


def draw_cluster(key, part):
    return routing(key)


def draw_embeddings(key, part):
    groups = routing(key)
    key = jax.random.fold_in(key, 3)
    key_centre, key_noise, key_spread, key_scale = jax.random.split(key, 4)
    centres = jax.random.normal(key_centre, (CLUSTERS, EMB), jnp.float32)
    noise = jax.random.normal(key_noise, (ROWS, EMB), jnp.float32)
    scale = jnp.exp(jax.random.uniform(key_scale, (ROWS, 1), jnp.float32, 0.0, math.log(10.0)))
    spread = jnp.exp(jax.random.uniform(key_spread, (ROWS, 1), jnp.float32, math.log(0.4), math.log(1.6)))
    rows = (centres[groups] + spread * noise) * scale
    return jnp.pad(rows, ((0, 0), (0, DP - EMB))).astype(jnp.bfloat16)


def draw_coords(key, part):
    key = jax.random.fold_in(key, 5)
    return jax.random.permutation(key, DP)[:KEEP].astype(jnp.int32)


def set_ends(entries, stream_key, smallest, top_value):
    index_at = [jax.random.randint(jax.random.fold_in(stream_key, axis), (), 0, length) for axis, length in enumerate(entries.shape)]
    longest = entries.shape.index(max(entries.shape))
    next_to = index_at[:longest] + [(index_at[longest] + 1) % entries.shape[longest]] + index_at[longest + 1:]
    return entries.at[tuple(index_at)].set(smallest).at[tuple(next_to)].set(top_value)


def setup_inputs(seed: int = 0) -> dict:
    keys = jax.random.split(jax.random.key(seed), 6)
    return {
        "embeddings": draw_embeddings(jax.random.fold_in(keys[5], 71), 0),
        "signs": set_ends(jax.random.randint(keys[1], (DP,), 0, 2), jax.random.fold_in(keys[1], 1), 0, 1).astype(jnp.int32),
        "coords": draw_coords(jax.random.fold_in(keys[5], 71), 0),
        "cluster": draw_cluster(jax.random.fold_in(keys[5], 71), 0),
        "order": jax.random.permutation(keys[4], ROWS).astype(jnp.int32),
    }


def walsh_rows(block):
    rows = block.shape[0]
    half = 1
    while half < DP:
        shaped = block.reshape(rows, DP // (2 * half), 2, half)
        block = jnp.stack((shaped[:, :, 0] + shaped[:, :, 1], shaped[:, :, 0] - shaped[:, :, 1]), axis=2).reshape(rows, DP)
        half = half * 2
    return block

def reference(embeddings, signs, coords, cluster, order):
    sign_row = (2 * signs - 1).astype(jnp.bfloat16)
    signed = embeddings * sign_row[None, :]

    def sketch_block(block):
        spread = walsh_rows(block.astype(jnp.float32))
        sketch = jnp.take(spread, coords, axis=1)
        total = lax.optimization_barrier(jnp.sum(sketch * sketch, axis=1, keepdims=True))
        return (sketch * lax.rsqrt(total + 1e-06)).astype(jnp.bfloat16)
    unit = lax.map(sketch_block, signed.reshape(OWNERS, ROW_DEV, DP)).reshape(ROWS, KEEP)
    owner = (cluster // CL_OWN).astype(jnp.int32)
    sorter = jnp.argsort(owner, stable=True).astype(jnp.int32)
    counts = jnp.zeros((OWNERS,), jnp.int32).at[owner].add(1)
    starts = (jnp.cumsum(counts) - counts).astype(jnp.int32)
    span = 4 * ROW_DEV
    sorted_unit = jnp.concatenate([unit[sorter], jnp.zeros((span, KEEP), jnp.bfloat16)], axis=0)
    sorted_cluster = jnp.concatenate([cluster[sorter], jnp.full((span,), -1, jnp.int32)], axis=0)
    sorted_order = jnp.concatenate([order[sorter], jnp.zeros((span,), jnp.int32)], axis=0)

    def per_owner(index):
        first = starts[index]
        queries = lax.dynamic_slice_in_dim(sorted_unit, first, span, 0)
        groups = lax.dynamic_slice_in_dim(sorted_cluster, first, span, 0)
        places = lax.dynamic_slice_in_dim(sorted_order, first, span, 0)
        scores = jnp.dot(queries, queries.T, preferred_element_type=jnp.float32)
        mask = (groups[None, :] == groups[:, None]) & (places[None, :] < places[:, None]) & (groups[None, :] >= 0)
        return lax.optimization_barrier(jnp.max(jnp.where(mask, scores, jnp.float32(0.0)), axis=1))
    table = lax.map(per_owner, jnp.arange(OWNERS, dtype=jnp.int32))
    sorted_owner = owner[sorter]
    local = jnp.arange(ROWS, dtype=jnp.int32) - starts[sorted_owner]
    values = table[sorted_owner, local]
    best = jnp.zeros((ROWS,), jnp.float32).at[sorter].set(values)
    return best.reshape(N_CLUS, N_FEAT * ROW_DEV)
```

```python
import functools

import jax
import jax.numpy as jnp
import numpy as np
from jax import lax
from jax.experimental import pallas as pl
from jax.experimental.pallas import tpu as pltpu
from jax.sharding import PartitionSpec as P

CL_OWN = 16


def walsh_table(count, dtype):
    index = np.arange(count)
    table = np.ones((count, count))
    for level in range(count.bit_length() - 1):
        both = (index[:, None] >> level & 1) * (index[None, :] >> level & 1)
        table = table * np.where(both == 1, -1.0, 1.0)
    return jnp.asarray(table, dtype)


def compare_rows(keys, key_cluster, key_order):
    total = keys.shape[0]
    block = 512
    steps = total // block

    def one_block(pieces):
        queries, groups, places = pieces
        scores = lax.dot_general(
            queries, keys, (((1,), (1,)), ((), ())), preferred_element_type=jnp.float32
        )
        mask = (
            (key_cluster[None, :] == groups[:, None])
            & (key_order[None, :] < places[:, None])
            & (key_cluster[None, :] >= 0)
        )
        return jnp.max(jnp.where(mask, scores, jnp.float32(0.0)), axis=1)

    parts_in = (
        keys.reshape(steps, block, keys.shape[1]),
        key_cluster.reshape(steps, block),
        key_order.reshape(steps, block),
    )
    return lax.map(one_block, parts_in).reshape(total)


def general(embeddings, signs, coords, cluster, order):
    feat_count = lax.axis_size("feat")
    clus_count = lax.axis_size("clus")
    owners = feat_count * clus_count
    rows_here = embeddings.shape[0] // feat_count
    width = embeddings.shape[1]
    total_dim = width * feat_count
    keep = coords.shape[0]
    capacity = 4 * rows_here // owners
    sign_row = (2 * signs - 1).astype(jnp.bfloat16)
    signed = embeddings * sign_row[None, :]
    inner = walsh_table(width, jnp.bfloat16)
    feat_index = lax.axis_index("feat")
    moved = lax.all_to_all(signed, "feat", split_axis=0, concat_axis=1, tiled=True)
    blocks = moved.reshape(rows_here, feat_count, width)
    partial_value = jnp.einsum("rab,bc->rac", blocks, inner, preferred_element_type=jnp.float32)
    outer = walsh_table(feat_count, jnp.float32)
    spread = jnp.einsum(
        "rab,ad->rdb", partial_value, outer, precision=lax.Precision.HIGHEST
    ).reshape(rows_here, total_dim)
    sketch = jnp.take(spread, coords, axis=1)
    total_sq = jnp.sum(sketch * sketch, axis=1, keepdims=True)
    unit = (sketch * lax.rsqrt(total_sq + 1e-06)).astype(jnp.bfloat16)
    mine = lax.dynamic_slice_in_dim(cluster, feat_index * rows_here, rows_here, 0)
    places = lax.dynamic_slice_in_dim(order, feat_index * rows_here, rows_here, 0)
    owner = mine // CL_OWN
    onehot = (owner[:, None] == jnp.arange(owners, dtype=jnp.int32)[None, :]).astype(jnp.bfloat16)
    line = jnp.arange(rows_here, dtype=jnp.int32)
    earlier = (line[:, None] > line[None, :]).astype(jnp.bfloat16)
    before = jnp.dot(earlier, onehot, preferred_element_type=jnp.float32)
    position = jnp.sum(before * onehot.astype(jnp.float32), axis=1).astype(jnp.int32)
    slot = owner * capacity + position
    sent = jnp.zeros((owners * capacity, keep), jnp.bfloat16).at[slot].set(unit)
    sent_cluster = jnp.full((owners * capacity,), -1, jnp.int32).at[slot].set(mine)
    sent_order = jnp.zeros((owners * capacity,), jnp.int32).at[slot].set(places)
    sent = sent.reshape(feat_count, clus_count, capacity, keep)
    sent_cluster = sent_cluster.reshape(feat_count, clus_count, capacity)
    sent_order = sent_order.reshape(feat_count, clus_count, capacity)
    arrived = (
        lax.all_to_all(
            lax.all_to_all(sent, "feat", split_axis=0, concat_axis=0, tiled=True),
            "clus",
            split_axis=1,
            concat_axis=1,
            tiled=True,
        ),
        lax.all_to_all(
            lax.all_to_all(sent_cluster, "feat", split_axis=0, concat_axis=0, tiled=True),
            "clus",
            split_axis=1,
            concat_axis=1,
            tiled=True,
        ),
        lax.all_to_all(
            lax.all_to_all(sent_order, "feat", split_axis=0, concat_axis=0, tiled=True),
            "clus",
            split_axis=1,
            concat_axis=1,
            tiled=True,
        ),
    )
    keys = arrived[0].reshape(owners * capacity, keep)
    arrived_cluster = arrived[1].reshape(owners * capacity)
    arrived_order = arrived[2].reshape(owners * capacity)
    scores = compare_rows(keys, arrived_cluster, arrived_order)
    scores = scores.reshape(feat_count, clus_count, capacity)
    returned = lax.all_to_all(
        lax.all_to_all(scores, "feat", split_axis=0, concat_axis=0, tiled=True),
        "clus",
        split_axis=1,
        concat_axis=1,
        tiled=True,
    )
    values = returned.reshape(owners * capacity)[slot]
    return values.reshape(1, rows_here)


LIVE = 5
RELAY = 6
PLACES = 32
DEVS = LIVE * PLACES
HALVES = 2
SLOTS = 720
TILE = 144
ROOM = 80
KEEP = 512
WIDTH = 256
GROUP = 6144
HALF = GROUP // HALVES
HERE = 768
COMPACT = HALVES * SLOTS
RECORDS = PLACES * ROOM
STRIDE = 4096
ORDER_BITS = 18
BATCH = 4
MESH_ID = pl.DeviceIdType.MESH
RELAYED = ((0, 3), (0, 4), (1, 4), (3, 0), (4, 0), (4, 1))
RELAY_ORDER = (1, 4, 2, 3, 0, 5)
BF = jnp.bfloat16
F32 = jnp.float32
I32 = jnp.int32
NT = (((1,), (1,)), ((), ()))


def iota(shape, dim):
    return lax.broadcasted_iota(I32, shape, dim)


def pick(mask):
    return jnp.where(mask, jnp.float32(1), jnp.float32(0)).astype(BF)


def dot(a, b):
    return jnp.dot(a, b, preferred_element_type=F32)


def dot_nt(a, b):
    return lax.dot_general(a, b, NT, preferred_element_type=F32)


def fast_kernel(
    x_ref, signs_ref, coords_ref, cluster_ref, order_ref,
    out_ref, flag_ref,
    key_ref, dev_ref, rank_ref, meta_ref, cm_ref, had_ref,
    sb_ref, rb_ref, relay_ref, unit_ref, s2_ref, r2_ref, sm_ref, rm_ref,
    best_ref, rs_ref, rr_ref, tg_ref,
    zs_sem, zr_sem, ys_sem, yr_sem, us_sem, ur_sem, ms_sem, mr_sem, bs_sem, br_sem, ts_sem, tr_sem, own_sem,
):
    z = lax.axis_index("feat")
    c = lax.axis_index("clus")
    live = z < LIVE
    barrier = pltpu.get_barrier_semaphore()
    for s in range(LIVE):
        @pl.when(z != s)
        def _():
            pl.semaphore_signal(barrier, inc=1, device_id={"feat": s}, device_id_type=MESH_ID)

    @pl.when((z == 0) | (z == 1) | (z == 3) | (z == 4))
    def _():
        pl.semaphore_signal(barrier, inc=1, device_id={"feat": RELAY}, device_id_type=MESH_ID)

    @pl.when(live)
    def _():
        def greet(i, carry):
            pl.semaphore_signal(barrier, inc=1, device_id={"clus": lax.rem(c + i, PLACES)}, device_id_type=MESH_ID)
            return carry
        lax.fori_loop(1, PLACES, greet, 0)

    meta_ref[...] = jnp.zeros_like(meta_ref)
    upper = pick(iota((WIDTH, WIDTH + 128), 0) < jnp.where(iota((WIDTH, WIDTH + 128), 1) < WIDTH, iota((WIDTH, WIDTH + 128), 1), WIDTH))
    classes = DEVS + 8

    def rank_block(b, base):
        at = pl.ds(pl.multiple_of(b * WIDTH, WIDTH), WIDTH)
        cl = cluster_ref[0:1, at]
        place = order_ref[0:1, at]
        spread = (cl >> 4) + 63 * (cl & 15)
        dev = spread - DEVS * ((spread.astype(F32) + 0.5) * (1.0 / DEVS)).astype(I32)
        q = ((dev.astype(F32) + 0.5) * (1.0 / LIVE)).astype(I32)
        plane = dev - LIVE * q
        line = iota((classes, WIDTH), 0)
        member = jnp.where((line == dev) | (line == plane + DEVS), jnp.float32(1), jnp.float32(0))
        counts = dot(member.astype(BF), upper)
        before = member * (counts[:, :WIDTH] + jnp.concatenate([base, base], axis=1))
        rank = jnp.sum(before[:DEVS], axis=0, keepdims=True).astype(I32)
        slot = jnp.sum(before[DEVS:], axis=0, keepdims=True).astype(I32)
        key_ref[0:1, at] = plane * STRIDE + slot
        dev_ref[0:1, at] = plane * PLACES + q
        rank_ref[0:1, at] = rank
        key = (cl << ORDER_BITS) + place
        row = iota((16, WIDTH), 0)
        info = jnp.where(row == 0, key & 255, 0)
        info = jnp.where(row == 1, (key >> 8) & 255, info)
        info = jnp.where(row == 2, (key >> 16) & 255, info)
        info = jnp.where(row == 3, (key >> 24) & 255, info)
        info = jnp.where(row == 4, 1, info)
        info = jnp.where(row == 5, q, info)
        info = jnp.where(row == 6, rank, info)
        meta_ref[0:16, at] = info.astype(F32).astype(BF)
        return base + counts[:, WIDTH:]

    base = jnp.zeros((classes, 128), F32)
    most = jnp.zeros((8, 128), F32)
    per_half = HALF // WIDTH
    for h in range(HALVES):
        base = lax.fori_loop(h * per_half, (h + 1) * per_half, rank_block, base)
        most = jnp.maximum(most, base[DEVS:])
        base = jnp.concatenate([base[:DEVS], jnp.zeros((8, 128), F32)], axis=0)
    over = jnp.where(jnp.max(most) > SLOTS, jnp.float32(1), jnp.float32(0))
    over = jnp.maximum(over, jnp.where(jnp.max(base[:DEVS]) > ROOM, jnp.float32(1), jnp.float32(0)))

    @pl.when(live)
    def _():
        pl.semaphore_wait(barrier, 7 + PLACES - 1)

    @pl.when(z == RELAY)
    def _():
        pl.semaphore_wait(barrier, 4)

    def target(i):
        down = 4 - i
        down = jnp.where(down <= z, down - 1, down)
        up = jnp.where(i >= z, i + 1, i)
        return jnp.where(z < 2, down, up)

    def far(p):
        return (p - z >= 3) | (z - p >= 3)

    def relay_slot(p):
        return jnp.where(p > z, z + p - 3, z + p)

    def direct_copy(i, h, p):
        return pltpu.make_async_remote_copy(
            src_ref=sb_ref.at[i, h], dst_ref=rb_ref.at[h, z],
            send_sem=zs_sem.at[i, h], recv_sem=zr_sem.at[h, z],
            device_id={"feat": p}, device_id_type=MESH_ID)

    def relay_copy(i, h, p):
        slot = relay_slot(p)
        return pltpu.make_async_remote_copy(
            src_ref=sb_ref.at[i, h], dst_ref=relay_ref.at[slot, h],
            send_sem=zs_sem.at[i, h], recv_sem=yr_sem.at[slot, h],
            device_id={"feat": RELAY}, device_id_type=MESH_ID)

    def forward_copy(r, h):
        src, dst = RELAYED[r]
        return pltpu.make_async_remote_copy(
            src_ref=relay_ref.at[r, h], dst_ref=rb_ref.at[h, src],
            send_sem=ys_sem.at[r, h], recv_sem=zr_sem.at[h, src],
            device_id={"feat": dst}, device_id_type=MESH_ID)

    def unit_copy(q):
        return pltpu.make_async_remote_copy(
            src_ref=s2_ref.at[q], dst_ref=r2_ref.at[c],
            send_sem=us_sem.at[q], recv_sem=ur_sem.at[c],
            device_id={"clus": q}, device_id_type=MESH_ID)

    def meta_copy(q):
        return pltpu.make_async_remote_copy(
            src_ref=sm_ref.at[q], dst_ref=rm_ref.at[c],
            send_sem=ms_sem.at[q], recv_sem=mr_sem.at[c],
            device_id={"clus": q}, device_id_type=MESH_ID)

    def best_copy(q):
        return pltpu.make_async_remote_copy(
            src_ref=rs_ref.at[q], dst_ref=rr_ref.at[c],
            send_sem=bs_sem.at[q], recv_sem=br_sem.at[c],
            device_id={"clus": q}, device_id_type=MESH_ID)

    def table_copy(p):
        return pltpu.make_async_remote_copy(
            src_ref=tg_ref.at[z], dst_ref=tg_ref.at[z],
            send_sem=ts_sem.at[p], recv_sem=tr_sem.at[z],
            device_id={"feat": p}, device_id_type=MESH_ID)

    def arrival(ref, sem, index):
        return pltpu.make_async_copy(ref.at[index], ref.at[index], sem.at[index])

    @pl.when(live)
    def _():
        sign = (2 * signs_ref[...] - 1).astype(F32)

        def chosen(h, p, t):
            keys = key_ref[0:1, h * HALF:(h + 1) * HALF]
            return pick(keys == iota((TILE, HALF), 0) + (p * STRIDE + t * TILE))

        for h in range(HALVES):
            def send_chunk(i, carry, h=h):
                p = target(i)

                def tile(t, carry):
                    rows = dot(chosen(h, p, t), x_ref[h * HALF:(h + 1) * HALF, :])
                    sb_ref[i, h, pl.ds(pl.multiple_of(t * TILE, TILE), TILE), :] = (rows * sign).astype(BF)
                    return carry
                lax.fori_loop(0, SLOTS // TILE, tile, 0)

                @pl.when(far(p))
                def _():
                    relay_copy(i, h, p).start()

                @pl.when(jnp.logical_not(far(p)))
                def _():
                    direct_copy(i, h, p).start()
                return carry
            lax.fori_loop(0, LIVE - 1, send_chunk, 0)

        for h in range(HALVES):
            def own(t, carry, h=h):
                at = pl.ds(pl.multiple_of(t * TILE, TILE), TILE)
                hot = chosen(h, z, t)
                rows = dot(hot, x_ref[h * HALF:(h + 1) * HALF, :])
                rb_ref[h, z, at, :] = (rows * sign).astype(BF)
                info = dot_nt(hot, meta_ref[:, h * HALF:(h + 1) * HALF])
                cm_ref[pl.ds(pl.multiple_of(h * SLOTS + t * TILE, TILE), TILE), :] = info.astype(BF)
                return carry
            lax.fori_loop(0, SLOTS // TILE, own, 0)

        unit16 = pick(iota((16, 128), 0) == iota((16, 128), 1))
        lanes = dot_nt(unit16, cm_ref[...])
        goal = jnp.where(lanes[4:5] > 0.5, lanes[5:6] * ROOM + lanes[6:7], -1.0).astype(I32)

        def placed(g):
            return pick(goal == iota((BATCH * ROOM, COMPACT), 0) + g * (BATCH * ROOM))

        def batch_of(i):
            return lax.rem(lax.div(c, BATCH) + 1 + i, PLACES // BATCH)

        def send_all(copy, g, source, sink, sem):
            def one(k, carry):
                q = g * BATCH + k

                @pl.when(q != c)
                def _():
                    copy(q).start()

                @pl.when(q == c)
                def _():
                    own_copy = pltpu.make_async_copy(source.at[q], sink.at[q], sem)
                    own_copy.start()
                    own_copy.wait()
                return carry
            lax.fori_loop(0, BATCH, one, 0)

        def send_meta(i, carry):
            g = batch_of(i)
            info = dot(placed(g), cm_ref[...])
            info = jnp.where(iota(info.shape, 1) == 5, over, info)
            sm_ref[pl.ds(g * BATCH, BATCH)] = info.astype(BF).reshape(BATCH, ROOM, 128)
            send_all(meta_copy, g, sm_ref, rm_ref, own_sem)
            return carry
        lax.fori_loop(0, PLACES // BATCH, send_meta, 0)

        def walsh(t, carry):
            at = pl.ds(pl.multiple_of(t * 128, 128), 128)
            both = (iota((128, KEEP), 0) + t * 128) & coords_ref[...]
            both = both ^ (both >> 8)
            both = both ^ (both >> 4)
            both = both ^ (both >> 2)
            both = both ^ (both >> 1)
            had_ref[at, :] = (1 - 2 * (both & 1)).astype(F32).astype(BF)
            return carry
        lax.fori_loop(0, LIVE * WIDTH // 128, walsh, 0)

        for h in range(HALVES):
            for s in range(LIVE):
                @pl.when(z != s)
                def _():
                    pltpu.make_async_copy(rb_ref.at[h, s], rb_ref.at[h, s], zr_sem.at[h, s]).wait()

            def transform(t, carry, h=h):
                at = pl.ds(pl.multiple_of(t * TILE, TILE), TILE)
                block = jnp.concatenate([rb_ref[h, s, at, :] for s in range(LIVE)], axis=1)
                sketch = dot(block, had_ref[...])
                total = jnp.sum(sketch * sketch, axis=1, keepdims=True)
                unit = sketch * lax.rsqrt(total + 1e-06)
                unit_ref[pl.ds(pl.multiple_of(h * SLOTS + t * TILE, TILE), TILE), :] = unit.astype(BF)
                return carry
            lax.fori_loop(0, SLOTS // TILE, transform, 0)

        def send_unit(i, carry):
            g = batch_of(i)
            rows = dot(placed(g), unit_ref[...])
            s2_ref[pl.ds(g * BATCH, BATCH)] = rows.astype(BF).reshape(BATCH, ROOM, KEEP)
            send_all(unit_copy, g, s2_ref, r2_ref, own_sem)
            return carry
        lax.fori_loop(0, PLACES // BATCH, send_unit, 0)

        def others(action):
            def one(i, carry):
                action(lax.rem(c + i, PLACES))
                return carry
            lax.fori_loop(1, PLACES, one, 0)

        others(lambda q: arrival(rm_ref, mr_sem, q).wait())
        others(lambda q: arrival(r2_ref, ur_sem, q).wait())

        lanes = dot_nt(unit16, rm_ref[...].reshape(RECORDS, 128))
        low = (lanes[0:1] + 256.0 * lanes[1:2] + 65536.0 * lanes[2:3]).astype(I32)
        query_key = low + (lanes[3:4].astype(I32) << 24)
        query_low = (query_key >> ORDER_BITS) << ORDER_BITS
        flag = jnp.max(lanes[5:6])
        many = 8 * ROOM
        wide = 512
        for t in range(RECORDS // wide):
            mine = query_key[:, t * wide:(t + 1) * wide]
            floor = query_low[:, t * wide:(t + 1) * wide]

            def compare(k, top, t=t, mine=mine, floor=floor):
                keys = r2_ref[pl.ds(k * 8, 8)].reshape(many, KEEP)
                info = rm_ref[pl.ds(k * 8, 8)].reshape(many, 128).astype(F32)
                key = (info[:, 0:1] + 256.0 * info[:, 1:2] + 65536.0 * info[:, 2:3]).astype(I32)
                key = key + (info[:, 3:4].astype(I32) << 24)
                key = jnp.where(info[:, 4:5] > 0.5, key, jnp.int32(2 ** 31 - 1))
                queries = r2_ref[...].reshape(RECORDS, KEEP)[t * wide:(t + 1) * wide]
                score = dot_nt(keys, queries)
                score = jnp.where((key < mine) & (key >= floor), score, 0.0)
                return jnp.maximum(top, jnp.max(score.reshape(many // 8, 8, wide), axis=0))
            top = lax.fori_loop(0, PLACES // 8, compare, jnp.zeros((8, wide), F32))
            best_ref[0:1, t * wide:(t + 1) * wide] = jnp.max(top, axis=0, keepdims=True)
        best_ref[0:1, RECORDS:] = jnp.zeros((1, 128), F32)

        for q in range(PLACES):
            start = q * ROOM // 128 * 128
            window = best_ref[0:1, start:start + 256]
            window = pltpu.roll(jnp.broadcast_to(window, (8, 256)), (256 - (q * ROOM - start)) % 256, 1)
            rs_ref[q] = window[:, :128]

        def send_best(q):
            best_copy(q).start()
        others(send_best)
        own_copy = pltpu.make_async_copy(rs_ref.at[c], rr_ref.at[c], own_sem)
        own_copy.start()
        own_copy.wait()
        others(lambda q: arrival(rr_ref, br_sem, q).wait())
        table = rr_ref[:, 0, :]
        tg_ref[z] = jnp.where(iota((PLACES, 128), 1) == 127, flag, table)
        for p in range(8):
            @pl.when(z != p)
            def _():
                table_copy(p).start()

        for h in range(HALVES):
            def sent(i, carry, h=h):
                direct_copy(i, h, target(i)).wait_send()
                return carry
            lax.fori_loop(0, LIVE - 1, sent, 0)
        others(lambda q: meta_copy(q).wait_send())
        others(lambda q: unit_copy(q).wait_send())
        others(lambda q: best_copy(q).wait_send())
        for p in range(8):
            @pl.when(z != p)
            def _():
                table_copy(p).wait_send()

    @pl.when(z == RELAY)
    def _():
        for h in range(HALVES):
            for r in RELAY_ORDER:
                pltpu.make_async_copy(relay_ref.at[r, h], relay_ref.at[r, h], yr_sem.at[r, h]).wait()
                forward_copy(r, h).start()
        for h in range(HALVES):
            for r in RELAY_ORDER:
                forward_copy(r, h).wait_send()

    for p in range(LIVE):
        @pl.when(z != p)
        def _():
            pltpu.make_async_copy(tg_ref.at[p], tg_ref.at[p], tr_sem.at[p]).wait()
    table = tg_ref[...].reshape(DEVS, 128)
    flag_ref[...] = jnp.broadcast_to(jnp.max(jnp.where(iota((DEVS, 128), 1) == 127, table, 0.0)), (1, 128))
    high = table.astype(BF)
    left = table - high.astype(F32)
    middle = left.astype(BF)
    lowest = (left - middle.astype(F32)).astype(BF)
    for t in range(HERE // WIDTH):
        at = pl.ds(pl.multiple_of(z * HERE + t * WIDTH, WIDTH), WIDTH)
        lane = pick(iota((128, WIDTH), 0) == rank_ref[0:1, at])
        found = dot(high, lane) + dot(middle, lane) + dot(lowest, lane)
        found = jnp.where(iota((DEVS, WIDTH), 0) == dev_ref[0:1, at], found, 0.0)
        out_ref[0:1, t * WIDTH:(t + 1) * WIDTH] = jnp.sum(found, axis=0, keepdims=True)


def local(embeddings, signs, coords, cluster, order):
    vmem = pl.BlockSpec(memory_space=pltpu.VMEM)
    dma = pltpu.SemaphoreType.DMA
    best, flag = pl.pallas_call(
        fast_kernel,
        out_shape=(jax.ShapeDtypeStruct((1, HERE), F32), jax.ShapeDtypeStruct((1, 128), F32)),
        in_specs=[vmem] * 5,
        out_specs=(vmem, vmem),
        scratch_shapes=[
            pltpu.VMEM((1, GROUP), I32),
            pltpu.VMEM((1, GROUP), I32),
            pltpu.VMEM((1, GROUP), I32),
            pltpu.VMEM((128, GROUP), BF),
            pltpu.VMEM((COMPACT, 128), BF),
            pltpu.VMEM((LIVE * WIDTH, KEEP), BF),
            pltpu.VMEM((LIVE - 1, HALVES, SLOTS, WIDTH), BF),
            pltpu.VMEM((HALVES, LIVE, SLOTS, WIDTH), BF),
            pltpu.VMEM((len(RELAYED), HALVES, SLOTS, WIDTH), BF),
            pltpu.VMEM((COMPACT, KEEP), BF),
            pltpu.VMEM((PLACES, ROOM, KEEP), BF),
            pltpu.VMEM((PLACES, ROOM, KEEP), BF),
            pltpu.VMEM((PLACES, ROOM, 128), BF),
            pltpu.VMEM((PLACES, ROOM, 128), BF),
            pltpu.VMEM((1, RECORDS + 128), F32),
            pltpu.VMEM((PLACES, 8, 128), F32),
            pltpu.VMEM((PLACES, 8, 128), F32),
            pltpu.VMEM((LIVE, PLACES, 128), F32),
            dma((LIVE - 1, HALVES)),
            dma((HALVES, LIVE)),
            dma((len(RELAYED), HALVES)),
            dma((len(RELAYED), HALVES)),
            dma((PLACES,)),
            dma((PLACES,)),
            dma((PLACES,)),
            dma((PLACES,)),
            dma((PLACES,)),
            dma((PLACES,)),
            dma((8,)),
            dma((LIVE,)),
            dma,
        ],
        compiler_params=pltpu.CompilerParams(
            collective_id=0, has_side_effects=True, vmem_limit_bytes=56 * 1024 * 1024
        ),
    )(
        embeddings,
        signs.reshape(1, WIDTH),
        coords.reshape(1, KEEP),
        cluster.reshape(1, GROUP),
        order.reshape(1, GROUP),
    )
    return lax.cond(
        flag[0, 0] > 0.5,
        lambda: general(embeddings, signs, coords, cluster, order),
        lambda: best,
    )


def solution(mesh):
    return jax.shard_map(
        local,
        mesh=mesh,
        in_specs=(P("clus", "feat"), P("feat"), P(), P("clus"), P("clus")),
        out_specs=P("clus", "feat"),
        check_vma=False,
    )
```

```python
import functools

import jax
import jax.numpy as jnp
import numpy as np
from jax import lax
from jax.experimental import pallas as pl
from jax.experimental.pallas import tpu as pltpu
from jax.sharding import PartitionSpec as P

CL_OWN = 16


def walsh_table(count, dtype):
    index = np.arange(count)
    table = np.ones((count, count))
    for level in range(count.bit_length() - 1):
        both = (index[:, None] >> level & 1) * (index[None, :] >> level & 1)
        table = table * np.where(both == 1, -1.0, 1.0)
    return jnp.asarray(table, dtype)


def compare_rows(keys, key_cluster, key_order):
    total = keys.shape[0]
    block = 512
    steps = total // block

    def one_block(pieces):
        queries, groups, places = pieces
        scores = lax.dot_general(
            queries, keys, (((1,), (1,)), ((), ())), preferred_element_type=jnp.float32
        )
        mask = (
            (key_cluster[None, :] == groups[:, None])
            & (key_order[None, :] < places[:, None])
            & (key_cluster[None, :] >= 0)
        )
        return jnp.max(jnp.where(mask, scores, jnp.float32(0.0)), axis=1)

    parts_in = (
        keys.reshape(steps, block, keys.shape[1]),
        key_cluster.reshape(steps, block),
        key_order.reshape(steps, block),
    )
    return lax.map(one_block, parts_in).reshape(total)


def general(embeddings, signs, coords, cluster, order):
    feat_count = lax.axis_size("feat")
    clus_count = lax.axis_size("clus")
    owners = feat_count * clus_count
    rows_here = embeddings.shape[0] // feat_count
    width = embeddings.shape[1]
    total_dim = width * feat_count
    keep = coords.shape[0]
    capacity = 4 * rows_here // owners
    sign_row = (2 * signs - 1).astype(jnp.bfloat16)
    signed = embeddings * sign_row[None, :]
    inner = walsh_table(width, jnp.bfloat16)
    feat_index = lax.axis_index("feat")
    moved = lax.all_to_all(signed, "feat", split_axis=0, concat_axis=1, tiled=True)
    blocks = moved.reshape(rows_here, feat_count, width)
    partial_value = jnp.einsum("rab,bc->rac", blocks, inner, preferred_element_type=jnp.float32)
    outer = walsh_table(feat_count, jnp.float32)
    spread = jnp.einsum(
        "rab,ad->rdb", partial_value, outer, precision=lax.Precision.HIGHEST
    ).reshape(rows_here, total_dim)
    sketch = jnp.take(spread, coords, axis=1)
    total_sq = jnp.sum(sketch * sketch, axis=1, keepdims=True)
    unit = (sketch * lax.rsqrt(total_sq + 1e-06)).astype(jnp.bfloat16)
    mine = lax.dynamic_slice_in_dim(cluster, feat_index * rows_here, rows_here, 0)
    places = lax.dynamic_slice_in_dim(order, feat_index * rows_here, rows_here, 0)
    owner = mine // CL_OWN
    onehot = (owner[:, None] == jnp.arange(owners, dtype=jnp.int32)[None, :]).astype(jnp.bfloat16)
    line = jnp.arange(rows_here, dtype=jnp.int32)
    earlier = (line[:, None] > line[None, :]).astype(jnp.bfloat16)
    before = jnp.dot(earlier, onehot, preferred_element_type=jnp.float32)
    position = jnp.sum(before * onehot.astype(jnp.float32), axis=1).astype(jnp.int32)
    slot = owner * capacity + position
    sent = jnp.zeros((owners * capacity, keep), jnp.bfloat16).at[slot].set(unit)
    sent_cluster = jnp.full((owners * capacity,), -1, jnp.int32).at[slot].set(mine)
    sent_order = jnp.zeros((owners * capacity,), jnp.int32).at[slot].set(places)
    sent = sent.reshape(feat_count, clus_count, capacity, keep)
    sent_cluster = sent_cluster.reshape(feat_count, clus_count, capacity)
    sent_order = sent_order.reshape(feat_count, clus_count, capacity)
    arrived = (
        lax.all_to_all(
            lax.all_to_all(sent, "feat", split_axis=0, concat_axis=0, tiled=True),
            "clus",
            split_axis=1,
            concat_axis=1,
            tiled=True,
        ),
        lax.all_to_all(
            lax.all_to_all(sent_cluster, "feat", split_axis=0, concat_axis=0, tiled=True),
            "clus",
            split_axis=1,
            concat_axis=1,
            tiled=True,
        ),
        lax.all_to_all(
            lax.all_to_all(sent_order, "feat", split_axis=0, concat_axis=0, tiled=True),
            "clus",
            split_axis=1,
            concat_axis=1,
            tiled=True,
        ),
    )
    keys = arrived[0].reshape(owners * capacity, keep)
    arrived_cluster = arrived[1].reshape(owners * capacity)
    arrived_order = arrived[2].reshape(owners * capacity)
    scores = compare_rows(keys, arrived_cluster, arrived_order)
    scores = scores.reshape(feat_count, clus_count, capacity)
    returned = lax.all_to_all(
        lax.all_to_all(scores, "feat", split_axis=0, concat_axis=0, tiled=True),
        "clus",
        split_axis=1,
        concat_axis=1,
        tiled=True,
    )
    values = returned.reshape(owners * capacity)[slot]
    return values.reshape(1, rows_here)


LIVE = 5
RELAY = 6
PLACES = 32
DEVS = LIVE * PLACES
HALVES = 2
SLOTS = 720
TILE = 144
TILES = SLOTS // TILE
ROOM = 48
KEEP = 512
WIDTH = 256
GROUP = 6144
HALF = GROUP // HALVES
HERE = 768
STRIDE = 4096
ORDER_BITS = 18
BATCH = 8
BATCHES = PLACES // BATCH
ROWS = BATCH * ROOM
FILLED = 256
BLOCKS = HALVES * BATCHES


def near(step):
    return min(step, 4 - step)


def far_first():
    steps = [(y, x, k) for y in range(4) for x in range(4) for k in range(2)]
    steps = sorted(steps[1:], key=lambda s: (-((s[0] == 2) + (s[1] == 2)), -near(s[0]) - near(s[1])))
    order = [(0, 0, 0)]
    for s in steps:
        for one in (s, (-s[0] % 4, -s[1] % 4, s[2])):
            if one not in order:
                order.append(one)
    return order


STEPS = far_first()
MESH_ID = pl.DeviceIdType.MESH
RELAYED = ((0, 3), (0, 4), (1, 4), (3, 0), (4, 0), (4, 1))
RELAY_ORDER = (1, 4, 2, 3, 0, 5)
BF = jnp.bfloat16
F32 = jnp.float32
I32 = jnp.int32
NT = (((1,), (1,)), ((), ()))


def iota(shape, dim):
    return lax.broadcasted_iota(I32, shape, dim)


def pick(mask):
    return jnp.where(mask, jnp.float32(1), jnp.float32(0)).astype(BF)


def dot(a, b):
    return jnp.dot(a, b, preferred_element_type=F32)


def dot_nt(a, b):
    return lax.dot_general(a, b, NT, preferred_element_type=F32)


def fast_kernel(
    x_ref, signs_ref, coords_ref, cluster_ref, order_ref,
    out_ref, flag_ref,
    key_ref, dev_ref, rank_ref, meta_ref, cm_ref, had_ref,
    sb_ref, rb_ref, relay_ref, unit_ref, s2_ref, r2_ref, sm_ref, rm_ref,
    pos_ref, full_ref, col_ref, row_ref, top_ref, best_ref, rs_ref, rr_ref, tg_ref,
    zs_sem, zr_sem, ys_sem, yr_sem, us_sem, ur_sem, ms_sem, mr_sem, bs_sem, br_sem, ts_sem, tr_sem, own_sem,
):
    z = lax.axis_index("feat")
    c = lax.axis_index("clus")
    live = z < LIVE
    barrier = pltpu.get_barrier_semaphore()
    for s in range(LIVE):
        @pl.when(z != s)
        def _():
            pl.semaphore_signal(barrier, inc=1, device_id={"feat": s}, device_id_type=MESH_ID)

    @pl.when((z == 0) | (z == 1) | (z == 3) | (z == 4))
    def _():
        pl.semaphore_signal(barrier, inc=1, device_id={"feat": RELAY}, device_id_type=MESH_ID)

    @pl.when(live)
    def _():
        def greet(i, carry):
            pl.semaphore_signal(barrier, inc=1, device_id={"clus": lax.rem(c + i, PLACES)}, device_id_type=MESH_ID)
            return carry
        lax.fori_loop(1, PLACES, greet, 0)

    meta_ref[...] = jnp.zeros_like(meta_ref)
    upper = pick(iota((WIDTH, WIDTH + 128), 0) < jnp.where(iota((WIDTH, WIDTH + 128), 1) < WIDTH, iota((WIDTH, WIDTH + 128), 1), WIDTH))
    classes = DEVS + 8

    def rank_block(h, b, base):
        at = pl.ds(pl.multiple_of(b * WIDTH, WIDTH), WIDTH)
        cl = cluster_ref[0:1, at]
        place = order_ref[0:1, at]
        spread = (cl >> 4) + 63 * (cl & 15)
        dev = spread - DEVS * ((spread.astype(F32) + 0.5) * (1.0 / DEVS)).astype(I32)
        q = ((dev.astype(F32) + 0.5) * (1.0 / LIVE)).astype(I32)
        plane = dev - LIVE * q
        line = iota((classes, WIDTH), 0)
        member = jnp.where((line == dev) | (line == plane + DEVS), jnp.float32(1), jnp.float32(0))
        counts = dot(member.astype(BF), upper)
        before = member * (counts[:, :WIDTH] + jnp.concatenate([base, base], axis=1))
        rank = jnp.sum(before[:DEVS], axis=0, keepdims=True).astype(I32)
        slot = jnp.sum(before[DEVS:], axis=0, keepdims=True).astype(I32)
        key_ref[0:1, at] = plane * STRIDE + slot
        dev_ref[0:1, at] = plane * PLACES + q
        rank_ref[0:1, at] = rank + h * ROOM
        key = (cl << ORDER_BITS) + place
        row = iota((16, WIDTH), 0)
        info = jnp.where(row == 0, key & 255, 0)
        info = jnp.where(row == 1, (key >> 8) & 255, info)
        info = jnp.where(row == 2, (key >> 16) & 255, info)
        info = jnp.where(row == 3, (key >> 24) & 255, info)
        info = jnp.where(row == 4, 1, info)
        info = jnp.where(row == 5, q, info)
        info = jnp.where(row == 6, rank, info)
        meta_ref[0:16, at] = info.astype(F32).astype(BF)
        return base + counts[:, WIDTH:]

    per_half = HALF // WIDTH

    def rank_half(h):
        count = lax.fori_loop(
            h * per_half, (h + 1) * per_half, functools.partial(rank_block, h), jnp.zeros((classes, 128), F32), unroll=3
        )
        crowded = jnp.where(jnp.max(count[DEVS:]) > SLOTS, jnp.float32(1), jnp.float32(0))
        return jnp.maximum(crowded, jnp.where(jnp.max(count[:DEVS]) > ROOM, jnp.float32(1), jnp.float32(0)))

    over = rank_half(0)

    @pl.when(live)
    def _():
        pl.semaphore_wait(barrier, 7 + PLACES - 1)

    @pl.when(z == RELAY)
    def _():
        pl.semaphore_wait(barrier, 4)

    def target(i):
        down = 4 - i
        down = jnp.where(down <= z, down - 1, down)
        up = jnp.where(i >= z, i + 1, i)
        return jnp.where(z < 2, down, up)

    def far(p):
        return (p - z >= 3) | (z - p >= 3)

    def relay_slot(p):
        return jnp.where(p > z, z + p - 3, z + p)

    def rows_of(t):
        return pl.ds(pl.multiple_of(t * TILE, TILE), TILE)

    def direct_copy(i, h, t, p):
        return pltpu.make_async_remote_copy(
            src_ref=sb_ref.at[i, h, rows_of(t)], dst_ref=rb_ref.at[h, z, rows_of(t)],
            send_sem=zs_sem.at[i, h, t], recv_sem=zr_sem.at[h, z, t],
            device_id={"feat": p}, device_id_type=MESH_ID)

    def relay_copy(i, h, t, p):
        slot = relay_slot(p)
        return pltpu.make_async_remote_copy(
            src_ref=sb_ref.at[i, h, rows_of(t)], dst_ref=relay_ref.at[slot, h, rows_of(t)],
            send_sem=zs_sem.at[i, h, t], recv_sem=yr_sem.at[slot, h, t],
            device_id={"feat": RELAY}, device_id_type=MESH_ID)

    def forward_copy(r, h, t):
        src, dst = RELAYED[r]
        return pltpu.make_async_remote_copy(
            src_ref=relay_ref.at[r, h, rows_of(t)], dst_ref=rb_ref.at[h, src, rows_of(t)],
            send_sem=ys_sem.at[r, h, t], recv_sem=zr_sem.at[h, src, t],
            device_id={"feat": dst}, device_id_type=MESH_ID)

    def seat(j, sign):
        y, x, k = STEPS[j]
        y = lax.rem(c // 8 + (4 + sign * y), 4)
        x = lax.rem(c // 2 % 4 + (4 + sign * x), 4)
        return y * 8 + x * 2 + lax.rem(c + k, 2)

    def unit_copy(h, j):
        q = seat(j, 1)
        return pltpu.make_async_remote_copy(
            src_ref=s2_ref.at[h, q], dst_ref=r2_ref.at[h, j],
            send_sem=us_sem.at[h, j], recv_sem=ur_sem.at[h, j],
            device_id={"clus": q}, device_id_type=MESH_ID)

    def meta_copy(j):
        q = seat(j, 1)
        return pltpu.make_async_remote_copy(
            src_ref=sm_ref.at[q], dst_ref=rm_ref.at[j],
            send_sem=ms_sem.at[j], recv_sem=mr_sem.at[j],
            device_id={"clus": q}, device_id_type=MESH_ID)

    def best_copy(j):
        q = seat(j, -1)
        return pltpu.make_async_remote_copy(
            src_ref=rs_ref.at[j], dst_ref=rr_ref.at[c],
            send_sem=bs_sem.at[j], recv_sem=br_sem.at[c],
            device_id={"clus": q}, device_id_type=MESH_ID)

    def table_copy(p):
        return pltpu.make_async_remote_copy(
            src_ref=tg_ref.at[z], dst_ref=tg_ref.at[z],
            send_sem=ts_sem.at[p], recv_sem=tr_sem.at[z],
            device_id={"feat": p}, device_id_type=MESH_ID)

    def arrival(ref, sem, *index):
        return pltpu.make_async_copy(ref.at[index], ref.at[index], sem.at[index])

    def others(action):
        def one(i, carry):
            action(lax.rem(c + i, PLACES))
            return carry
        lax.fori_loop(1, PLACES, one, 0)

    def chosen(h, p, t):
        keys = key_ref[0:1, h * HALF:(h + 1) * HALF]
        return pick(keys == iota((TILE, HALF), 0) + (p * STRIDE + t * TILE))

    sign = (2 * signs_ref[...] - 1).astype(F32)

    def send_half(h):
        def send_tile(k, carry):
            t = k // (LIVE - 1)
            i = k % (LIVE - 1)
            p = target(i)
            rows = dot(chosen(h, p, t), x_ref[h * HALF:(h + 1) * HALF, :])
            sb_ref[i, h, rows_of(t), :] = (rows * sign).astype(BF)

            @pl.when(far(p))
            def _():
                relay_copy(i, h, t, p).start()

            @pl.when(jnp.logical_not(far(p)))
            def _():
                direct_copy(i, h, t, p).start()
            return carry
        lax.fori_loop(0, TILES * (LIVE - 1), send_tile, 0)

    @pl.when(live)
    def _():
        send_half(0)

    over = jnp.maximum(over, rank_half(1))

    @pl.when(live)
    def _():
        send_half(1)

        for h in range(HALVES):
            def own(t, carry, h=h):
                hot = chosen(h, z, t)
                rows = dot(hot, x_ref[h * HALF:(h + 1) * HALF, :])
                rb_ref[h, z, rows_of(t), :] = (rows * sign).astype(BF)
                cm_ref[h, rows_of(t), :] = dot_nt(hot, meta_ref[:, h * HALF:(h + 1) * HALF]).astype(BF)
                return carry
            lax.fori_loop(0, TILES, own, 0)

        def walsh(t, carry):
            at = pl.ds(pl.multiple_of(t * 128, 128), 128)
            both = (iota((128, KEEP), 0) + t * 128) & coords_ref[...]
            both = both ^ (both >> 8)
            both = both ^ (both >> 4)
            both = both ^ (both >> 2)
            both = both ^ (both >> 1)
            had_ref[at, :] = (1 - 2 * (both & 1)).astype(F32).astype(BF)
            return carry
        lax.fori_loop(0, LIVE * WIDTH // 128, walsh, 0)

        unit16 = pick(iota((16, 128), 0) == iota((16, 128), 1))

        def goal_of(h):
            lanes = dot_nt(unit16, cm_ref[h])
            return jnp.where(lanes[4:5] > 0.5, lanes[5:6] * ROOM + lanes[6:7], -1.0).astype(I32)
        goals = [goal_of(h) for h in range(HALVES)]

        def placed(h, g):
            return pick(goals[h] == iota((ROWS, SLOTS), 0) + g * ROWS)

        def send_meta(g, carry):
            for h in range(HALVES):
                info = dot(placed(h, g), cm_ref[h])
                info = jnp.where(iota(info.shape, 1) == 5, over, info)
                sm_ref[pl.ds(g * BATCH, BATCH), h] = info.astype(BF).reshape(BATCH, ROOM, 128)
            return carry
        lax.fori_loop(0, BATCHES, send_meta, 0)

        def keep_own(source, sink):
            own_copy = pltpu.make_async_copy(source, sink, own_sem)
            own_copy.start()
            return own_copy
        kept = keep_own(sm_ref.at[c], rm_ref.at[0])
        for j in range(1, PLACES):
            meta_copy(j).start()
        kept.wait()

        def transform(h):
            def tile(t, carry):
                for s in range(LIVE):
                    @pl.when(z != s)
                    def _():
                        arrived = rb_ref.at[h, s, rows_of(t)]
                        pltpu.make_async_copy(arrived, arrived, zr_sem.at[h, s, t]).wait()
                block = jnp.concatenate([rb_ref[h, s, rows_of(t), :] for s in range(LIVE)], axis=1)
                sketch = dot(block, had_ref[...])
                total = jnp.sum(sketch * sketch, axis=1, keepdims=True)
                unit_ref[h, rows_of(t), :] = (sketch * lax.rsqrt(total + 1e-06)).astype(BF)
                return carry
            lax.fori_loop(0, TILES, tile, 0)

        def send_units(h):
            def one(g, carry):
                rows = dot(placed(h, g), unit_ref[h])
                s2_ref[h, pl.ds(g * BATCH, BATCH)] = rows.astype(BF).reshape(BATCH, ROOM, KEEP)
                return carry
            lax.fori_loop(0, BATCHES, one, 0)
            for j in range(1, PLACES):
                unit_copy(h, j).start()
            keep_own(s2_ref.at[h, c], r2_ref.at[h, 0]).wait()

        before = pick(iota((ROWS, ROWS), 0) < iota((ROWS, ROWS), 1))

        def read_meta(b, carry):
            h = b // BATCHES
            info = rm_ref[pl.ds(lax.rem(b, BATCHES) * BATCH, BATCH), h].reshape(ROWS, 128)
            lanes = dot_nt(unit16, info)
            flag, most = carry
            rank = dot(lanes.astype(BF), before)[4:5]
            flag = jnp.maximum(flag, jnp.max(lanes[5:6]))
            most = jnp.maximum(most, jnp.max(rank + lanes[4:5]))
            position = jnp.where(lanes[4:5] > 0.5, rank, -1.0).astype(I32)
            pos_ref[b] = jnp.broadcast_to(position, (8, ROWS))
            packed = dot(pick(position == iota((FILLED, ROWS), 0)), info)
            key = (packed[:, 0:1] + 256.0 * packed[:, 1:2] + 65536.0 * packed[:, 2:3]).astype(I32)
            key = key + (packed[:, 3:4].astype(I32) << 24)
            key = jnp.where(packed[:, 4:5] > 0.5, key, jnp.int32(2 ** 31 - 1))
            col_ref[b] = jnp.broadcast_to(key, (FILLED, 128))
            lanes = dot_nt(unit16, packed.astype(BF))
            key = (lanes[0:1] + 256.0 * lanes[1:2] + 65536.0 * lanes[2:3]).astype(I32)
            row_ref[b] = jnp.broadcast_to(key + (lanes[3:4].astype(I32) << 24), (8, FILLED))
            return flag, most

        def pack(h, k):
            for j in range(k * BATCH, (k + 1) * BATCH):
                if j:
                    arrival(r2_ref, ur_sem, h, j).wait()
            b = h * BATCHES + k
            rows = r2_ref[h, k * BATCH:(k + 1) * BATCH].reshape(ROWS, KEEP)
            full_ref[b] = dot(pick(pos_ref[b, 0:1] == iota((FILLED, ROWS), 0)), rows).astype(BF)

        def match(i, k):
            mine = row_ref[i, 0:1]
            floor = (mine >> ORDER_BITS) << ORDER_BITS
            key = col_ref[k]
            key = jnp.concatenate([key, key], axis=1)
            score = dot_nt(full_ref[k], full_ref[i])
            score = jnp.where((key < mine) & (key >= floor), score, 0.0)
            return jnp.max(score.reshape(FILLED // 8, 8, FILLED), axis=0)

        def compare(b):
            def queries(k, top):
                return jnp.maximum(top, match(b, k))
            top_ref[b] = lax.fori_loop(0, b + 1, queries, jnp.zeros((8, FILLED), F32), unroll=True)

            def candidates(i, carry):
                top_ref[i] = jnp.maximum(top_ref[i], match(i, b))
                return carry
            lax.fori_loop(0, b, candidates, 0, unroll=True)

        transform(0)
        send_units(0)
        for j in range(1, PLACES):
            arrival(rm_ref, mr_sem, j).wait()
        flag, most = lax.fori_loop(0, BLOCKS, read_meta, (jnp.float32(0), jnp.float32(0)))
        flag = jnp.maximum(flag, jnp.where(most > FILLED, jnp.float32(1), jnp.float32(0)))
        for k in range(BATCHES):
            pack(0, k)
            compare(k)
        transform(1)
        send_units(1)
        for k in range(BATCHES):
            pack(1, k)
            compare(BATCHES + k)
        for b in range(BLOCKS):
            top = jnp.max(top_ref[b], axis=0, keepdims=True)
            high = top.astype(BF).astype(F32)
            middle = (top - high).astype(BF).astype(F32)
            line = iota((16, FILLED), 0)
            parts = jnp.where(line == 0, high, jnp.where(line == 1, middle, jnp.where(line == 2, top - high - middle, 0.0)))
            parts = dot(parts.astype(BF), pick(iota((FILLED, ROWS), 0) == pos_ref[b, 0:1]))
            best_ref[b, :, :ROWS] = jnp.broadcast_to(parts[0:1] + parts[1:2] + parts[2:3], (8, ROWS))
            best_ref[b, :, ROWS:] = jnp.zeros((8, 128), F32)

        for j in range(PLACES):
            start = j % BATCH * ROOM
            left = start // 128 * 128
            pieces = []
            for h in range(HALVES):
                window = best_ref[h * BATCHES + j // BATCH, :, left:left + 256]
                pieces.append(pltpu.roll(window, (256 - (start - left) + h * ROOM) % 256, 1)[:, :128])
            lane = iota((8, 128), 1)
            rs_ref[j] = jnp.where(lane == 127, flag, jnp.where(lane < ROOM, pieces[0], pieces[1]))
            if j:
                best_copy(j).start()
        keep_own(rs_ref.at[0], rr_ref.at[c]).wait()
        others(lambda q: arrival(rr_ref, br_sem, q).wait())
        table = rr_ref[:, 0, :]
        tg_ref[z] = table
        for p in range(8):
            @pl.when(z != p)
            def _():
                table_copy(p).start()

        for h in range(HALVES):
            def sent(k, carry, h=h):
                direct_copy(k % (LIVE - 1), h, k // (LIVE - 1), target(k % (LIVE - 1))).wait_send()
                return carry
            lax.fori_loop(0, TILES * (LIVE - 1), sent, 0)
            for j in range(1, PLACES):
                unit_copy(h, j).wait_send()
        for j in range(1, PLACES):
            meta_copy(j).wait_send()
            best_copy(j).wait_send()
        for p in range(8):
            @pl.when(z != p)
            def _():
                table_copy(p).wait_send()

    @pl.when(z == RELAY)
    def _():
        for h in range(HALVES):
            def forward(t, carry, h=h):
                for r in RELAY_ORDER:
                    held = relay_ref.at[r, h, rows_of(t)]
                    pltpu.make_async_copy(held, held, yr_sem.at[r, h, t]).wait()
                    forward_copy(r, h, t).start()
                return carry
            lax.fori_loop(0, TILES, forward, 0)
        for h in range(HALVES):
            def forwarded(t, carry, h=h):
                for r in RELAY_ORDER:
                    forward_copy(r, h, t).wait_send()
                return carry
            lax.fori_loop(0, TILES, forwarded, 0)

    for p in range(LIVE):
        @pl.when(z != p)
        def _():
            pltpu.make_async_copy(tg_ref.at[p], tg_ref.at[p], tr_sem.at[p]).wait()
    table = tg_ref[...].reshape(DEVS, 128)
    flag_ref[...] = jnp.broadcast_to(jnp.max(jnp.where(iota((DEVS, 128), 1) == 127, table, 0.0)), (1, 128))
    high = table.astype(BF)
    left = table - high.astype(F32)
    middle = left.astype(BF)
    lowest = (left - middle.astype(F32)).astype(BF)
    for t in range(HERE // WIDTH):
        at = pl.ds(pl.multiple_of(z * HERE + t * WIDTH, WIDTH), WIDTH)
        lane = pick(iota((128, WIDTH), 0) == rank_ref[0:1, at])
        found = dot(high, lane) + dot(middle, lane) + dot(lowest, lane)
        found = jnp.where(iota((DEVS, WIDTH), 0) == dev_ref[0:1, at], found, 0.0)
        out_ref[0:1, t * WIDTH:(t + 1) * WIDTH] = jnp.sum(found, axis=0, keepdims=True)


def local(embeddings, signs, coords, cluster, order):
    vmem = pl.BlockSpec(memory_space=pltpu.VMEM)
    dma = pltpu.SemaphoreType.DMA
    best, flag = pl.pallas_call(
        fast_kernel,
        out_shape=(jax.ShapeDtypeStruct((1, HERE), F32), jax.ShapeDtypeStruct((1, 128), F32)),
        in_specs=[vmem] * 5,
        out_specs=(vmem, vmem),
        scratch_shapes=[
            pltpu.VMEM((1, GROUP), I32),
            pltpu.VMEM((1, GROUP), I32),
            pltpu.VMEM((1, GROUP), I32),
            pltpu.VMEM((128, GROUP), BF),
            pltpu.VMEM((HALVES, SLOTS, 128), BF),
            pltpu.VMEM((LIVE * WIDTH, KEEP), BF),
            pltpu.VMEM((LIVE - 1, HALVES, SLOTS, WIDTH), BF),
            pltpu.VMEM((HALVES, LIVE, SLOTS, WIDTH), BF),
            pltpu.VMEM((len(RELAYED), HALVES, SLOTS, WIDTH), BF),
            pltpu.VMEM((HALVES, SLOTS, KEEP), BF),
            pltpu.VMEM((HALVES, PLACES, ROOM, KEEP), BF),
            pltpu.VMEM((HALVES, PLACES, ROOM, KEEP), BF),
            pltpu.VMEM((PLACES, HALVES, ROOM, 128), BF),
            pltpu.VMEM((PLACES, HALVES, ROOM, 128), BF),
            pltpu.VMEM((BLOCKS, 8, ROWS), I32),
            pltpu.VMEM((BLOCKS, FILLED, KEEP), BF),
            pltpu.VMEM((BLOCKS, FILLED, 128), I32),
            pltpu.VMEM((BLOCKS, 8, FILLED), I32),
            pltpu.VMEM((BLOCKS, 8, FILLED), F32),
            pltpu.VMEM((BLOCKS, 8, ROWS + 128), F32),
            pltpu.VMEM((PLACES, 8, 128), F32),
            pltpu.VMEM((PLACES, 8, 128), F32),
            pltpu.VMEM((LIVE, PLACES, 128), F32),
            dma((LIVE - 1, HALVES, TILES)),
            dma((HALVES, LIVE, TILES)),
            dma((len(RELAYED), HALVES, TILES)),
            dma((len(RELAYED), HALVES, TILES)),
            dma((HALVES, PLACES)),
            dma((HALVES, PLACES)),
            dma((PLACES,)),
            dma((PLACES,)),
            dma((PLACES,)),
            dma((PLACES,)),
            dma((8,)),
            dma((LIVE,)),
            dma,
        ],
        compiler_params=pltpu.CompilerParams(
            collective_id=0, has_side_effects=True, vmem_limit_bytes=56 * 1024 * 1024
        ),
    )(
        embeddings,
        signs.reshape(1, WIDTH),
        coords.reshape(1, KEEP),
        cluster.reshape(1, GROUP),
        order.reshape(1, GROUP),
    )
    return lax.cond(
        flag[0, 0] > 0.5,
        lambda: general(embeddings, signs, coords, cluster, order),
        lambda: best,
    )


def solution(mesh):
    return jax.shard_map(
        local,
        mesh=mesh,
        in_specs=(P("clus", "feat"), P("feat"), P(), P("clus"), P("clus")),
        out_specs=P("clus", "feat"),
        check_vma=False,
    )
```

```python
import functools

import jax
import jax.numpy as jnp
import numpy as np
from jax import lax
from jax.experimental import pallas as pl
from jax.experimental.pallas import tpu as pltpu
from jax.sharding import PartitionSpec as P

CL_OWN = 16


def walsh_table(count, dtype):
    index = np.arange(count)
    table = np.ones((count, count))
    for level in range(count.bit_length() - 1):
        both = (index[:, None] >> level & 1) * (index[None, :] >> level & 1)
        table = table * np.where(both == 1, -1.0, 1.0)
    return jnp.asarray(table, dtype)


def compare_rows(keys, key_cluster, key_order):
    total = keys.shape[0]
    block = 512
    steps = total // block

    def one_block(pieces):
        queries, groups, places = pieces
        scores = lax.dot_general(
            queries, keys, (((1,), (1,)), ((), ())), preferred_element_type=jnp.float32
        )
        mask = (
            (key_cluster[None, :] == groups[:, None])
            & (key_order[None, :] < places[:, None])
            & (key_cluster[None, :] >= 0)
        )
        return jnp.max(jnp.where(mask, scores, jnp.float32(0.0)), axis=1)

    parts_in = (
        keys.reshape(steps, block, keys.shape[1]),
        key_cluster.reshape(steps, block),
        key_order.reshape(steps, block),
    )
    return lax.map(one_block, parts_in).reshape(total)


def general(embeddings, signs, coords, cluster, order):
    feat_count = lax.axis_size("feat")
    clus_count = lax.axis_size("clus")
    owners = feat_count * clus_count
    rows_here = embeddings.shape[0] // feat_count
    width = embeddings.shape[1]
    total_dim = width * feat_count
    keep = coords.shape[0]
    capacity = 4 * rows_here // owners
    sign_row = (2 * signs - 1).astype(jnp.bfloat16)
    signed = embeddings * sign_row[None, :]
    inner = walsh_table(width, jnp.bfloat16)
    feat_index = lax.axis_index("feat")
    moved = lax.all_to_all(signed, "feat", split_axis=0, concat_axis=1, tiled=True)
    blocks = moved.reshape(rows_here, feat_count, width)
    partial_value = jnp.einsum("rab,bc->rac", blocks, inner, preferred_element_type=jnp.float32)
    outer = walsh_table(feat_count, jnp.float32)
    spread = jnp.einsum(
        "rab,ad->rdb", partial_value, outer, precision=lax.Precision.HIGHEST
    ).reshape(rows_here, total_dim)
    sketch = jnp.take(spread, coords, axis=1)
    total_sq = jnp.sum(sketch * sketch, axis=1, keepdims=True)
    unit = (sketch * lax.rsqrt(total_sq + 1e-06)).astype(jnp.bfloat16)
    mine = lax.dynamic_slice_in_dim(cluster, feat_index * rows_here, rows_here, 0)
    places = lax.dynamic_slice_in_dim(order, feat_index * rows_here, rows_here, 0)
    owner = mine // CL_OWN
    onehot = (owner[:, None] == jnp.arange(owners, dtype=jnp.int32)[None, :]).astype(jnp.bfloat16)
    line = jnp.arange(rows_here, dtype=jnp.int32)
    earlier = (line[:, None] > line[None, :]).astype(jnp.bfloat16)
    before = jnp.dot(earlier, onehot, preferred_element_type=jnp.float32)
    position = jnp.sum(before * onehot.astype(jnp.float32), axis=1).astype(jnp.int32)
    slot = owner * capacity + position
    sent = jnp.zeros((owners * capacity, keep), jnp.bfloat16).at[slot].set(unit)
    sent_cluster = jnp.full((owners * capacity,), -1, jnp.int32).at[slot].set(mine)
    sent_order = jnp.zeros((owners * capacity,), jnp.int32).at[slot].set(places)
    sent = sent.reshape(feat_count, clus_count, capacity, keep)
    sent_cluster = sent_cluster.reshape(feat_count, clus_count, capacity)
    sent_order = sent_order.reshape(feat_count, clus_count, capacity)
    arrived = (
        lax.all_to_all(
            lax.all_to_all(sent, "feat", split_axis=0, concat_axis=0, tiled=True),
            "clus",
            split_axis=1,
            concat_axis=1,
            tiled=True,
        ),
        lax.all_to_all(
            lax.all_to_all(sent_cluster, "feat", split_axis=0, concat_axis=0, tiled=True),
            "clus",
            split_axis=1,
            concat_axis=1,
            tiled=True,
        ),
        lax.all_to_all(
            lax.all_to_all(sent_order, "feat", split_axis=0, concat_axis=0, tiled=True),
            "clus",
            split_axis=1,
            concat_axis=1,
            tiled=True,
        ),
    )
    keys = arrived[0].reshape(owners * capacity, keep)
    arrived_cluster = arrived[1].reshape(owners * capacity)
    arrived_order = arrived[2].reshape(owners * capacity)
    scores = compare_rows(keys, arrived_cluster, arrived_order)
    scores = scores.reshape(feat_count, clus_count, capacity)
    returned = lax.all_to_all(
        lax.all_to_all(scores, "feat", split_axis=0, concat_axis=0, tiled=True),
        "clus",
        split_axis=1,
        concat_axis=1,
        tiled=True,
    )
    values = returned.reshape(owners * capacity)[slot]
    return values.reshape(1, rows_here)


LIVE = 5
PLACES = 32
DEVS = LIVE * PLACES
HALVES = 2
SLOTS = 720
TILE = 144
TILES = SLOTS // TILE
ROOM = 48
STRAIGHT = 1
KEEP = 512
WIDTH = 256
GROUP = 6144
HALF = GROUP // HALVES
HERE = 768
STRIDE = 4096
ORDER_BITS = 18
BATCH = 8
BATCHES = PLACES // BATCH
ROWS = BATCH * ROOM
FILLED = 256
BLOCKS = HALVES * BATCHES


def near(step):
    return min(step, 4 - step)


def far_first():
    steps = [(y, x, k) for y in range(4) for x in range(4) for k in range(2)]
    steps = sorted(steps[1:], key=lambda s: (-((s[0] == 2) + (s[1] == 2)), -near(s[0]) - near(s[1])))
    order = [(0, 0, 0)]
    for s in steps:
        for one in (s, (-s[0] % 4, -s[1] % 4, s[2])):
            if one not in order:
                order.append(one)
    return order


STEPS = far_first()
MESH_ID = pl.DeviceIdType.MESH
BF = jnp.bfloat16
F32 = jnp.float32
I32 = jnp.int32
NT = (((1,), (1,)), ((), ()))


def iota(shape, dim):
    return lax.broadcasted_iota(I32, shape, dim)


def pick(mask):
    return jnp.where(mask, jnp.float32(1), jnp.float32(0)).astype(BF)


def dot(a, b):
    return jnp.dot(a, b, preferred_element_type=F32)


def dot_nt(a, b):
    return lax.dot_general(a, b, NT, preferred_element_type=F32)


def fast_kernel(
    x_ref, signs_ref, coords_ref, cluster_ref, order_ref,
    out_ref, flag_ref,
    key_ref, dev_ref, rank_ref, meta_ref, cm_ref, had_ref,
    sb_ref, rb_ref, relay_ref, unit_ref, s2_ref, r2_ref, sm_ref, rm_ref,
    pos_ref, full_ref, col_ref, row_ref, top_ref, best_ref, rs_ref, rr_ref, tg_ref,
    zs_sem, zr_sem, ys_sem, yr_sem, us_sem, ur_sem, ms_sem, mr_sem, bs_sem, br_sem, ts_sem, tr_sem, own_sem,
):
    z = lax.axis_index("feat")
    c = lax.axis_index("clus")
    live = z < LIVE
    barrier = pltpu.get_barrier_semaphore()
    for s in range(LIVE):
        @pl.when(z != s)
        def _():
            pl.semaphore_signal(barrier, inc=1, device_id={"feat": s}, device_id_type=MESH_ID)

    for a, b in ((0, 3), (0, 4), (1, 4)):
        @pl.when((z == a) | (z == b))
        def _():
            pl.semaphore_signal(barrier, inc=1, device_id={"feat": a + b + 2}, device_id_type=MESH_ID)

    @pl.when(live)
    def _():
        def greet(i, carry):
            pl.semaphore_signal(barrier, inc=1, device_id={"clus": lax.rem(c + i, PLACES)}, device_id_type=MESH_ID)
            return carry
        lax.fori_loop(1, PLACES, greet, 0)

    meta_ref[...] = jnp.zeros_like(meta_ref)
    upper = pick(iota((WIDTH, WIDTH + 128), 0) < jnp.where(iota((WIDTH, WIDTH + 128), 1) < WIDTH, iota((WIDTH, WIDTH + 128), 1), WIDTH))
    classes = DEVS + 8

    def rank_block(h, b, base):
        at = pl.ds(pl.multiple_of(b * WIDTH, WIDTH), WIDTH)
        cl = cluster_ref[0:1, at]
        place = order_ref[0:1, at]
        spread = (cl >> 4) + 63 * (cl & 15)
        dev = spread - DEVS * ((spread.astype(F32) + 0.5) * (1.0 / DEVS)).astype(I32)
        q = ((dev.astype(F32) + 0.5) * (1.0 / LIVE)).astype(I32)
        plane = dev - LIVE * q
        line = iota((classes, WIDTH), 0)
        member = jnp.where((line == dev) | (line == plane + DEVS), jnp.float32(1), jnp.float32(0))
        counts = dot(member.astype(BF), upper)
        before = member * (counts[:, :WIDTH] + jnp.concatenate([base, base], axis=1))
        rank = jnp.sum(before[:DEVS], axis=0, keepdims=True).astype(I32)
        slot = jnp.sum(before[DEVS:], axis=0, keepdims=True).astype(I32)
        key_ref[0:1, at] = plane * STRIDE + slot
        dev_ref[0:1, at] = plane * PLACES + q
        rank_ref[0:1, at] = rank + h * ROOM
        key = (cl << ORDER_BITS) + place
        row = iota((16, WIDTH), 0)
        info = jnp.where(row == 0, key & 255, 0)
        info = jnp.where(row == 1, (key >> 8) & 255, info)
        info = jnp.where(row == 2, (key >> 16) & 255, info)
        info = jnp.where(row == 3, (key >> 24) & 255, info)
        info = jnp.where(row == 4, 1, info)
        info = jnp.where(row == 5, q, info)
        info = jnp.where(row == 6, rank, info)
        meta_ref[0:16, at] = info.astype(F32).astype(BF)
        return base + counts[:, WIDTH:]

    per_half = HALF // WIDTH

    def rank_half(h):
        count = lax.fori_loop(
            h * per_half, (h + 1) * per_half, functools.partial(rank_block, h), jnp.zeros((classes, 128), F32), unroll=3
        )
        crowded = jnp.where(jnp.max(count[DEVS:]) > SLOTS, jnp.float32(1), jnp.float32(0))
        return jnp.maximum(crowded, jnp.where(jnp.max(count[:DEVS]) > ROOM, jnp.float32(1), jnp.float32(0)))

    over = rank_half(0)

    @pl.when(live)
    def _():
        pl.semaphore_wait(barrier, 7 + PLACES - 1)

    @pl.when(jnp.logical_not(live))
    def _():
        pl.semaphore_wait(barrier, 2)

    def target(i):
        down = 4 - i
        down = jnp.where(down <= z, down - 1, down)
        up = jnp.where(i >= z, i + 1, i)
        return jnp.where(z < 2, down, up)

    def far(p, h, t):
        steps = jnp.where(p > z, p - z, z - p)
        return (steps >= 4) | ((steps == 3) & (h * TILES + t < HALVES * TILES - STRAIGHT))

    def rows_of(t):
        return pl.ds(pl.multiple_of(t * TILE, TILE), TILE)

    def direct_copy(i, h, t, p):
        return pltpu.make_async_remote_copy(
            src_ref=sb_ref.at[i, h, rows_of(t)], dst_ref=rb_ref.at[h, z, rows_of(t)],
            send_sem=zs_sem.at[i, h, t], recv_sem=zr_sem.at[h, z, t],
            device_id={"feat": p}, device_id_type=MESH_ID)

    def relay_copy(i, h, t, p):
        slot = jnp.where(p > z, 0, 1)
        return pltpu.make_async_remote_copy(
            src_ref=sb_ref.at[i, h, rows_of(t)], dst_ref=relay_ref.at[slot, h, rows_of(t)],
            send_sem=zs_sem.at[i, h, t], recv_sem=yr_sem.at[slot, h, t],
            device_id={"feat": z + p + 2}, device_id_type=MESH_ID)

    def forward_copy(r, h, t):
        low = z // 7
        high = z - 2 - low
        src, dst = (low, high) if r == 0 else (high, low)
        return pltpu.make_async_remote_copy(
            src_ref=relay_ref.at[r, h, rows_of(t)], dst_ref=rb_ref.at[h, src, rows_of(t)],
            send_sem=ys_sem.at[r, h, t], recv_sem=zr_sem.at[h, src, t],
            device_id={"feat": dst}, device_id_type=MESH_ID)

    def seat(j, sign):
        y, x, k = STEPS[j]
        y = lax.rem(c // 8 + (4 + sign * y), 4)
        x = lax.rem(c // 2 % 4 + (4 + sign * x), 4)
        return y * 8 + x * 2 + lax.rem(c + k, 2)

    def unit_copy(h, j):
        q = seat(j, 1)
        return pltpu.make_async_remote_copy(
            src_ref=s2_ref.at[h, q], dst_ref=r2_ref.at[h, j],
            send_sem=us_sem.at[h, j], recv_sem=ur_sem.at[h, j],
            device_id={"clus": q}, device_id_type=MESH_ID)

    def meta_copy(j):
        q = seat(j, 1)
        return pltpu.make_async_remote_copy(
            src_ref=sm_ref.at[q], dst_ref=rm_ref.at[j],
            send_sem=ms_sem.at[j], recv_sem=mr_sem.at[j],
            device_id={"clus": q}, device_id_type=MESH_ID)

    def best_copy(j):
        q = seat(j, -1)
        return pltpu.make_async_remote_copy(
            src_ref=rs_ref.at[j], dst_ref=rr_ref.at[c],
            send_sem=bs_sem.at[j], recv_sem=br_sem.at[c],
            device_id={"clus": q}, device_id_type=MESH_ID)

    def table_copy(p):
        return pltpu.make_async_remote_copy(
            src_ref=tg_ref.at[z], dst_ref=tg_ref.at[z],
            send_sem=ts_sem.at[p], recv_sem=tr_sem.at[z],
            device_id={"feat": p}, device_id_type=MESH_ID)

    def arrival(ref, sem, *index):
        return pltpu.make_async_copy(ref.at[index], ref.at[index], sem.at[index])

    def others(action):
        def one(i, carry):
            action(lax.rem(c + i, PLACES))
            return carry
        lax.fori_loop(1, PLACES, one, 0)

    def chosen(h, p, t):
        keys = key_ref[0:1, h * HALF:(h + 1) * HALF]
        return pick(keys == iota((TILE, HALF), 0) + (p * STRIDE + t * TILE))

    sign = (2 * signs_ref[...] - 1).astype(F32)

    def send_half(h):
        def send_tile(k, carry):
            t = k // (LIVE - 1)
            i = k % (LIVE - 1)
            p = target(i)
            rows = dot(chosen(h, p, t), x_ref[h * HALF:(h + 1) * HALF, :])
            sb_ref[i, h, rows_of(t), :] = (rows * sign).astype(BF)

            @pl.when(far(p, h, t))
            def _():
                relay_copy(i, h, t, p).start()

            @pl.when(jnp.logical_not(far(p, h, t)))
            def _():
                direct_copy(i, h, t, p).start()
            return carry
        lax.fori_loop(0, TILES * (LIVE - 1), send_tile, 0)

    @pl.when(live)
    def _():
        send_half(0)

    over = jnp.maximum(over, rank_half(1))

    @pl.when(live)
    def _():
        send_half(1)

        for h in range(HALVES):
            def own(t, carry, h=h):
                hot = chosen(h, z, t)
                rows = dot(hot, x_ref[h * HALF:(h + 1) * HALF, :])
                rb_ref[h, z, rows_of(t), :] = (rows * sign).astype(BF)
                cm_ref[h, rows_of(t), :] = dot_nt(hot, meta_ref[:, h * HALF:(h + 1) * HALF]).astype(BF)
                return carry
            lax.fori_loop(0, TILES, own, 0)

        def walsh(t, carry):
            at = pl.ds(pl.multiple_of(t * 128, 128), 128)
            both = (iota((128, KEEP), 0) + t * 128) & coords_ref[...]
            both = both ^ (both >> 8)
            both = both ^ (both >> 4)
            both = both ^ (both >> 2)
            both = both ^ (both >> 1)
            had_ref[at, :] = (1 - 2 * (both & 1)).astype(F32).astype(BF)
            return carry
        lax.fori_loop(0, LIVE * WIDTH // 128, walsh, 0)

        unit16 = pick(iota((16, 128), 0) == iota((16, 128), 1))

        def goal_of(h):
            lanes = dot_nt(unit16, cm_ref[h])
            return jnp.where(lanes[4:5] > 0.5, lanes[5:6] * ROOM + lanes[6:7], -1.0).astype(I32)
        goals = [goal_of(h) for h in range(HALVES)]

        def placed(h, g):
            return pick(goals[h] == iota((ROWS, SLOTS), 0) + g * ROWS)

        def send_meta(g, carry):
            for h in range(HALVES):
                info = dot(placed(h, g), cm_ref[h])
                info = jnp.where(iota(info.shape, 1) == 5, over, info)
                sm_ref[pl.ds(g * BATCH, BATCH), h] = info.astype(BF).reshape(BATCH, ROOM, 128)
            return carry
        lax.fori_loop(0, BATCHES, send_meta, 0)

        def keep_own(source, sink):
            own_copy = pltpu.make_async_copy(source, sink, own_sem)
            own_copy.start()
            return own_copy
        kept = keep_own(sm_ref.at[c], rm_ref.at[0])
        for j in range(1, PLACES):
            meta_copy(j).start()
        kept.wait()

        def transform(h):
            def tile(t, carry):
                for s in range(LIVE):
                    @pl.when(z != s)
                    def _():
                        arrived = rb_ref.at[h, s, rows_of(t)]
                        pltpu.make_async_copy(arrived, arrived, zr_sem.at[h, s, t]).wait()
                block = jnp.concatenate([rb_ref[h, s, rows_of(t), :] for s in range(LIVE)], axis=1)
                sketch = dot(block, had_ref[...])
                total = jnp.sum(sketch * sketch, axis=1, keepdims=True)
                unit_ref[h, rows_of(t), :] = (sketch * lax.rsqrt(total + 1e-06)).astype(BF)
                return carry
            lax.fori_loop(0, TILES, tile, 0)

        def send_units(h):
            def one(g, carry):
                rows = dot(placed(h, g), unit_ref[h])
                s2_ref[h, pl.ds(g * BATCH, BATCH)] = rows.astype(BF).reshape(BATCH, ROOM, KEEP)
                return carry
            lax.fori_loop(0, BATCHES, one, 0)
            for j in range(1, PLACES):
                unit_copy(h, j).start()
            keep_own(s2_ref.at[h, c], r2_ref.at[h, 0]).wait()

        before = pick(iota((ROWS, ROWS), 0) < iota((ROWS, ROWS), 1))

        def read_meta(b, carry):
            h = b // BATCHES
            info = rm_ref[pl.ds(lax.rem(b, BATCHES) * BATCH, BATCH), h].reshape(ROWS, 128)
            lanes = dot_nt(unit16, info)
            flag, most = carry
            rank = dot(lanes.astype(BF), before)[4:5]
            flag = jnp.maximum(flag, jnp.max(lanes[5:6]))
            most = jnp.maximum(most, jnp.max(rank + lanes[4:5]))
            position = jnp.where(lanes[4:5] > 0.5, rank, -1.0).astype(I32)
            pos_ref[b] = jnp.broadcast_to(position, (8, ROWS))
            packed = dot(pick(position == iota((FILLED, ROWS), 0)), info)
            key = (packed[:, 0:1] + 256.0 * packed[:, 1:2] + 65536.0 * packed[:, 2:3]).astype(I32)
            key = key + (packed[:, 3:4].astype(I32) << 24)
            key = jnp.where(packed[:, 4:5] > 0.5, key, jnp.int32(2 ** 31 - 1))
            col_ref[b] = jnp.broadcast_to(key, (FILLED, 128))
            lanes = dot_nt(unit16, packed.astype(BF))
            key = (lanes[0:1] + 256.0 * lanes[1:2] + 65536.0 * lanes[2:3]).astype(I32)
            row_ref[b] = jnp.broadcast_to(key + (lanes[3:4].astype(I32) << 24), (8, FILLED))
            return flag, most

        def pack(h, k):
            for j in range(k * BATCH, (k + 1) * BATCH):
                if j:
                    arrival(r2_ref, ur_sem, h, j).wait()
            b = h * BATCHES + k
            rows = r2_ref[h, k * BATCH:(k + 1) * BATCH].reshape(ROWS, KEEP)
            full_ref[b] = dot(pick(pos_ref[b, 0:1] == iota((FILLED, ROWS), 0)), rows).astype(BF)

        def match(i, k):
            mine = row_ref[i, 0:1]
            floor = (mine >> ORDER_BITS) << ORDER_BITS
            key = col_ref[k]
            key = jnp.concatenate([key, key], axis=1)
            score = dot_nt(full_ref[k], full_ref[i])
            score = jnp.where((key < mine) & (key >= floor), score, 0.0)
            return jnp.max(score.reshape(FILLED // 8, 8, FILLED), axis=0)

        def compare(b):
            def queries(k, top):
                return jnp.maximum(top, match(b, k))
            top_ref[b] = lax.fori_loop(0, b + 1, queries, jnp.zeros((8, FILLED), F32), unroll=True)

            def candidates(i, carry):
                top_ref[i] = jnp.maximum(top_ref[i], match(i, b))
                return carry
            lax.fori_loop(0, b, candidates, 0, unroll=True)

        transform(0)
        send_units(0)
        transform(1)
        send_units(1)
        for j in range(1, PLACES):
            arrival(rm_ref, mr_sem, j).wait()
        flag, most = lax.fori_loop(0, BLOCKS, read_meta, (jnp.float32(0), jnp.float32(0)))
        flag = jnp.maximum(flag, jnp.where(most > FILLED, jnp.float32(1), jnp.float32(0)))
        for k in range(BATCHES):
            pack(0, k)
            compare(k)
        for k in range(BATCHES):
            pack(1, k)
            compare(BATCHES + k)
        for b in range(BLOCKS):
            top = jnp.max(top_ref[b], axis=0, keepdims=True)
            high = top.astype(BF).astype(F32)
            middle = (top - high).astype(BF).astype(F32)
            line = iota((16, FILLED), 0)
            parts = jnp.where(line == 0, high, jnp.where(line == 1, middle, jnp.where(line == 2, top - high - middle, 0.0)))
            parts = dot(parts.astype(BF), pick(iota((FILLED, ROWS), 0) == pos_ref[b, 0:1]))
            best_ref[b, :, :ROWS] = jnp.broadcast_to(parts[0:1] + parts[1:2] + parts[2:3], (8, ROWS))
            best_ref[b, :, ROWS:] = jnp.zeros((8, 128), F32)

        for j in range(PLACES):
            start = j % BATCH * ROOM
            left = start // 128 * 128
            pieces = []
            for h in range(HALVES):
                window = best_ref[h * BATCHES + j // BATCH, :, left:left + 256]
                pieces.append(pltpu.roll(window, (256 - (start - left) + h * ROOM) % 256, 1)[:, :128])
            lane = iota((8, 128), 1)
            rs_ref[j] = jnp.where(lane == 127, flag, jnp.where(lane < ROOM, pieces[0], pieces[1]))
            if j:
                best_copy(j).start()
        keep_own(rs_ref.at[0], rr_ref.at[c]).wait()
        others(lambda q: arrival(rr_ref, br_sem, q).wait())
        table = rr_ref[:, 0, :]
        tg_ref[z] = table
        for p in range(8):
            @pl.when(z != p)
            def _():
                table_copy(p).start()

        for h in range(HALVES):
            def sent(k, carry, h=h):
                direct_copy(k % (LIVE - 1), h, k // (LIVE - 1), target(k % (LIVE - 1))).wait_send()
                return carry
            lax.fori_loop(0, TILES * (LIVE - 1), sent, 0)
            for j in range(1, PLACES):
                unit_copy(h, j).wait_send()
        for j in range(1, PLACES):
            meta_copy(j).wait_send()
            best_copy(j).wait_send()
        for p in range(8):
            @pl.when(z != p)
            def _():
                table_copy(p).wait_send()

    @pl.when(jnp.logical_not(live))
    def _():
        def passed(r, h, t, action):
            @pl.when((z == 6) | (h * TILES + t < HALVES * TILES - STRAIGHT))
            def _():
                action(r, h, t)

        def pass_on(r, h, t):
            held = relay_ref.at[r, h, rows_of(t)]
            pltpu.make_async_copy(held, held, yr_sem.at[r, h, t]).wait()
            forward_copy(r, h, t).start()

        for action in (pass_on, lambda r, h, t: forward_copy(r, h, t).wait_send()):
            for h in range(HALVES):
                def tile(t, carry, h=h, action=action):
                    for r in range(2):
                        passed(r, h, t, action)
                    return carry
                lax.fori_loop(0, TILES, tile, 0)

    for p in range(LIVE):
        @pl.when(z != p)
        def _():
            pltpu.make_async_copy(tg_ref.at[p], tg_ref.at[p], tr_sem.at[p]).wait()
    table = tg_ref[...].reshape(DEVS, 128)
    flag_ref[...] = jnp.broadcast_to(jnp.max(jnp.where(iota((DEVS, 128), 1) == 127, table, 0.0)), (1, 128))
    high = table.astype(BF)
    left = table - high.astype(F32)
    middle = left.astype(BF)
    lowest = (left - middle.astype(F32)).astype(BF)
    for t in range(HERE // WIDTH):
        at = pl.ds(pl.multiple_of(z * HERE + t * WIDTH, WIDTH), WIDTH)
        lane = pick(iota((128, WIDTH), 0) == rank_ref[0:1, at])
        found = dot(high, lane) + dot(middle, lane) + dot(lowest, lane)
        found = jnp.where(iota((DEVS, WIDTH), 0) == dev_ref[0:1, at], found, 0.0)
        out_ref[0:1, t * WIDTH:(t + 1) * WIDTH] = jnp.sum(found, axis=0, keepdims=True)


def local(embeddings, signs, coords, cluster, order):
    vmem = pl.BlockSpec(memory_space=pltpu.VMEM)
    dma = pltpu.SemaphoreType.DMA
    best, flag = pl.pallas_call(
        fast_kernel,
        out_shape=(jax.ShapeDtypeStruct((1, HERE), F32), jax.ShapeDtypeStruct((1, 128), F32)),
        in_specs=[vmem] * 5,
        out_specs=(vmem, vmem),
        scratch_shapes=[
            pltpu.VMEM((1, GROUP), I32),
            pltpu.VMEM((1, GROUP), I32),
            pltpu.VMEM((1, GROUP), I32),
            pltpu.VMEM((128, GROUP), BF),
            pltpu.VMEM((HALVES, SLOTS, 128), BF),
            pltpu.VMEM((LIVE * WIDTH, KEEP), BF),
            pltpu.VMEM((LIVE - 1, HALVES, SLOTS, WIDTH), BF),
            pltpu.VMEM((HALVES, LIVE, SLOTS, WIDTH), BF),
            pltpu.VMEM((2, HALVES, SLOTS, WIDTH), BF),
            pltpu.VMEM((HALVES, SLOTS, KEEP), BF),
            pltpu.VMEM((HALVES, PLACES, ROOM, KEEP), BF),
            pltpu.VMEM((HALVES, PLACES, ROOM, KEEP), BF),
            pltpu.VMEM((PLACES, HALVES, ROOM, 128), BF),
            pltpu.VMEM((PLACES, HALVES, ROOM, 128), BF),
            pltpu.VMEM((BLOCKS, 8, ROWS), I32),
            pltpu.VMEM((BLOCKS, FILLED, KEEP), BF),
            pltpu.VMEM((BLOCKS, FILLED, 128), I32),
            pltpu.VMEM((BLOCKS, 8, FILLED), I32),
            pltpu.VMEM((BLOCKS, 8, FILLED), F32),
            pltpu.VMEM((BLOCKS, 8, ROWS + 128), F32),
            pltpu.VMEM((PLACES, 8, 128), F32),
            pltpu.VMEM((PLACES, 8, 128), F32),
            pltpu.VMEM((LIVE, PLACES, 128), F32),
            dma((LIVE - 1, HALVES, TILES)),
            dma((HALVES, LIVE, TILES)),
            dma((2, HALVES, TILES)),
            dma((2, HALVES, TILES)),
            dma((HALVES, PLACES)),
            dma((HALVES, PLACES)),
            dma((PLACES,)),
            dma((PLACES,)),
            dma((PLACES,)),
            dma((PLACES,)),
            dma((8,)),
            dma((LIVE,)),
            dma,
        ],
        compiler_params=pltpu.CompilerParams(
            collective_id=0, has_side_effects=True, vmem_limit_bytes=56 * 1024 * 1024
        ),
    )(
        embeddings,
        signs.reshape(1, WIDTH),
        coords.reshape(1, KEEP),
        cluster.reshape(1, GROUP),
        order.reshape(1, GROUP),
    )
    return lax.cond(
        flag[0, 0] > 0.5,
        lambda: general(embeddings, signs, coords, cluster, order),
        lambda: best,
    )


def solution(mesh):
    return jax.shard_map(
        local,
        mesh=mesh,
        in_specs=(P("clus", "feat"), P("feat"), P(), P("clus"), P("clus")),
        out_specs=P("clus", "feat"),
        check_vma=False,
    )
```

```python
import functools

import jax
import jax.numpy as jnp
import numpy as np
from jax import lax
from jax.experimental import pallas as pl
from jax.experimental.pallas import tpu as pltpu
from jax.sharding import PartitionSpec as P

CL_OWN = 16


def walsh_table(count, dtype):
    index = np.arange(count)
    table = np.ones((count, count))
    for level in range(count.bit_length() - 1):
        both = (index[:, None] >> level & 1) * (index[None, :] >> level & 1)
        table = table * np.where(both == 1, -1.0, 1.0)
    return jnp.asarray(table, dtype)


def compare_rows(keys, key_cluster, key_order):
    total = keys.shape[0]
    block = 512
    steps = total // block

    def one_block(pieces):
        queries, groups, places = pieces
        scores = lax.dot_general(
            queries, keys, (((1,), (1,)), ((), ())), preferred_element_type=jnp.float32
        )
        mask = (
            (key_cluster[None, :] == groups[:, None])
            & (key_order[None, :] < places[:, None])
            & (key_cluster[None, :] >= 0)
        )
        return jnp.max(jnp.where(mask, scores, jnp.float32(0.0)), axis=1)

    parts_in = (
        keys.reshape(steps, block, keys.shape[1]),
        key_cluster.reshape(steps, block),
        key_order.reshape(steps, block),
    )
    return lax.map(one_block, parts_in).reshape(total)


def general(embeddings, signs, coords, cluster, order):
    feat_count = lax.axis_size("feat")
    clus_count = lax.axis_size("clus")
    owners = feat_count * clus_count
    rows_here = embeddings.shape[0] // feat_count
    width = embeddings.shape[1]
    total_dim = width * feat_count
    keep = coords.shape[0]
    capacity = 4 * rows_here // owners
    sign_row = (2 * signs - 1).astype(jnp.bfloat16)
    signed = embeddings * sign_row[None, :]
    inner = walsh_table(width, jnp.bfloat16)
    feat_index = lax.axis_index("feat")
    moved = lax.all_to_all(signed, "feat", split_axis=0, concat_axis=1, tiled=True)
    blocks = moved.reshape(rows_here, feat_count, width)
    partial_value = jnp.einsum("rab,bc->rac", blocks, inner, preferred_element_type=jnp.float32)
    outer = walsh_table(feat_count, jnp.float32)
    spread = jnp.einsum(
        "rab,ad->rdb", partial_value, outer, precision=lax.Precision.HIGHEST
    ).reshape(rows_here, total_dim)
    sketch = jnp.take(spread, coords, axis=1)
    total_sq = jnp.sum(sketch * sketch, axis=1, keepdims=True)
    unit = (sketch * lax.rsqrt(total_sq + 1e-06)).astype(jnp.bfloat16)
    mine = lax.dynamic_slice_in_dim(cluster, feat_index * rows_here, rows_here, 0)
    places = lax.dynamic_slice_in_dim(order, feat_index * rows_here, rows_here, 0)
    owner = mine // CL_OWN
    onehot = (owner[:, None] == jnp.arange(owners, dtype=jnp.int32)[None, :]).astype(jnp.bfloat16)
    line = jnp.arange(rows_here, dtype=jnp.int32)
    earlier = (line[:, None] > line[None, :]).astype(jnp.bfloat16)
    before = jnp.dot(earlier, onehot, preferred_element_type=jnp.float32)
    position = jnp.sum(before * onehot.astype(jnp.float32), axis=1).astype(jnp.int32)
    slot = owner * capacity + position
    sent = jnp.zeros((owners * capacity, keep), jnp.bfloat16).at[slot].set(unit)
    sent_cluster = jnp.full((owners * capacity,), -1, jnp.int32).at[slot].set(mine)
    sent_order = jnp.zeros((owners * capacity,), jnp.int32).at[slot].set(places)
    sent = sent.reshape(feat_count, clus_count, capacity, keep)
    sent_cluster = sent_cluster.reshape(feat_count, clus_count, capacity)
    sent_order = sent_order.reshape(feat_count, clus_count, capacity)
    arrived = (
        lax.all_to_all(
            lax.all_to_all(sent, "feat", split_axis=0, concat_axis=0, tiled=True),
            "clus",
            split_axis=1,
            concat_axis=1,
            tiled=True,
        ),
        lax.all_to_all(
            lax.all_to_all(sent_cluster, "feat", split_axis=0, concat_axis=0, tiled=True),
            "clus",
            split_axis=1,
            concat_axis=1,
            tiled=True,
        ),
        lax.all_to_all(
            lax.all_to_all(sent_order, "feat", split_axis=0, concat_axis=0, tiled=True),
            "clus",
            split_axis=1,
            concat_axis=1,
            tiled=True,
        ),
    )
    keys = arrived[0].reshape(owners * capacity, keep)
    arrived_cluster = arrived[1].reshape(owners * capacity)
    arrived_order = arrived[2].reshape(owners * capacity)
    scores = compare_rows(keys, arrived_cluster, arrived_order)
    scores = scores.reshape(feat_count, clus_count, capacity)
    returned = lax.all_to_all(
        lax.all_to_all(scores, "feat", split_axis=0, concat_axis=0, tiled=True),
        "clus",
        split_axis=1,
        concat_axis=1,
        tiled=True,
    )
    values = returned.reshape(owners * capacity)[slot]
    return values.reshape(1, rows_here)


LIVE = 5
PLACES = 32
DEVS = LIVE * PLACES
HALVES = 2
SLOTS = 720
TILE = 144
TILES = SLOTS // TILE
ROOM = 48
STRAIGHT = 1
KEEP = 512
WIDTH = 256
GROUP = 6144
HALF = GROUP // HALVES
HERE = 768
STRIDE = 4096
ORDER_BITS = 18
BATCH = 8
BATCHES = PLACES // BATCH
ROWS = BATCH * ROOM
FILLED = 256
BLOCKS = HALVES * BATCHES


def near(step):
    return min(step, 4 - step)


def far_first():
    steps = [(y, x, k) for y in range(4) for x in range(4) for k in range(2)]
    steps = sorted(steps[1:], key=lambda s: (-((s[0] == 2) + (s[1] == 2)), -near(s[0]) - near(s[1])))
    order = [(0, 0, 0)]
    for s in steps:
        for one in (s, (-s[0] % 4, -s[1] % 4, s[2])):
            if one not in order:
                order.append(one)
    return order


STEPS = far_first()
MESH_ID = pl.DeviceIdType.MESH
BF = jnp.bfloat16
F32 = jnp.float32
I32 = jnp.int32
NT = (((1,), (1,)), ((), ()))


def iota(shape, dim):
    return lax.broadcasted_iota(I32, shape, dim)


def pick(mask):
    return jnp.where(mask, jnp.float32(1), jnp.float32(0)).astype(BF)


def dot(a, b):
    return jnp.dot(a, b, preferred_element_type=F32)


def dot_nt(a, b):
    return lax.dot_general(a, b, NT, preferred_element_type=F32)


def fast_kernel(
    hbm_ref, signs_ref, coords_ref, cluster_ref, order_ref,
    out_ref, flag_ref,
    key_ref, dev_ref, rank_ref, meta_ref, cm_ref, had_ref,
    sb_ref, rb_ref, relay_ref, unit_ref, s2_ref, r2_ref, sm_ref, rm_ref,
    pos_ref, full_ref, col_ref, row_ref, top_ref, best_ref, rs_ref, rr_ref, tg_ref,
    zs_sem, zr_sem, ys_sem, yr_sem, us_sem, ur_sem, ms_sem, mr_sem, bs_sem, br_sem, ts_sem, tr_sem, own_sem, x_ref, x_sem,
):
    z = lax.axis_index("feat")
    c = lax.axis_index("clus")
    live = z < LIVE
    barrier = pltpu.get_barrier_semaphore()
    fetch = pltpu.make_async_copy(hbm_ref, x_ref, x_sem)
    fetch.start()
    for s in range(LIVE):
        @pl.when(z != s)
        def _():
            pl.semaphore_signal(barrier, inc=1, device_id={"feat": s}, device_id_type=MESH_ID)

    for a, b in ((0, 3), (0, 4), (1, 4)):
        @pl.when((z == a) | (z == b))
        def _():
            pl.semaphore_signal(barrier, inc=1, device_id={"feat": a + b + 2}, device_id_type=MESH_ID)

    @pl.when(live)
    def _():
        def greet(i, carry):
            pl.semaphore_signal(barrier, inc=1, device_id={"clus": lax.rem(c + i, PLACES)}, device_id_type=MESH_ID)
            return carry
        lax.fori_loop(1, PLACES, greet, 0)

    meta_ref[...] = jnp.zeros_like(meta_ref)
    upper = pick(iota((WIDTH, WIDTH + 128), 0) < jnp.where(iota((WIDTH, WIDTH + 128), 1) < WIDTH, iota((WIDTH, WIDTH + 128), 1), WIDTH))
    classes = DEVS + 8

    def rank_block(h, b, base):
        at = pl.ds(pl.multiple_of(b * WIDTH, WIDTH), WIDTH)
        cl = cluster_ref[0:1, at]
        place = order_ref[0:1, at]
        spread = (cl >> 4) + 63 * (cl & 15)
        dev = spread - DEVS * ((spread.astype(F32) + 0.5) * (1.0 / DEVS)).astype(I32)
        q = ((dev.astype(F32) + 0.5) * (1.0 / LIVE)).astype(I32)
        plane = dev - LIVE * q
        line = iota((classes, WIDTH), 0)
        member = jnp.where((line == dev) | (line == plane + DEVS), jnp.float32(1), jnp.float32(0))
        counts = dot(member.astype(BF), upper)
        before = member * (counts[:, :WIDTH] + jnp.concatenate([base, base], axis=1))
        rank = jnp.sum(before[:DEVS], axis=0, keepdims=True).astype(I32)
        slot = jnp.sum(before[DEVS:], axis=0, keepdims=True).astype(I32)
        key_ref[0:1, at] = plane * STRIDE + slot
        dev_ref[0:1, at] = plane * PLACES + q
        rank_ref[0:1, at] = rank + h * ROOM
        key = (cl << ORDER_BITS) + place
        row = iota((16, WIDTH), 0)
        info = jnp.where(row == 0, key & 255, 0)
        info = jnp.where(row == 1, (key >> 8) & 255, info)
        info = jnp.where(row == 2, (key >> 16) & 255, info)
        info = jnp.where(row == 3, (key >> 24) & 255, info)
        info = jnp.where(row == 4, 1, info)
        info = jnp.where(row == 5, q, info)
        info = jnp.where(row == 6, rank, info)
        meta_ref[0:16, at] = info.astype(F32).astype(BF)
        return base + counts[:, WIDTH:]

    per_half = HALF // WIDTH

    def rank_half(h):
        count = lax.fori_loop(
            h * per_half, (h + 1) * per_half, functools.partial(rank_block, h), jnp.zeros((classes, 128), F32), unroll=3
        )
        crowded = jnp.where(jnp.max(count[DEVS:]) > SLOTS, jnp.float32(1), jnp.float32(0))
        return jnp.maximum(crowded, jnp.where(jnp.max(count[:DEVS]) > ROOM, jnp.float32(1), jnp.float32(0)))

    over = rank_half(0)
    fetch.wait()

    @pl.when(live)
    def _():
        pl.semaphore_wait(barrier, 7 + PLACES - 1)

    @pl.when(jnp.logical_not(live))
    def _():
        pl.semaphore_wait(barrier, 2)

    def target(i):
        down = 4 - i
        down = jnp.where(down <= z, down - 1, down)
        up = jnp.where(i >= z, i + 1, i)
        return jnp.where(z < 2, down, up)

    def far(p, h, t):
        steps = jnp.where(p > z, p - z, z - p)
        return (steps >= 4) | ((steps == 3) & (h * TILES + t < HALVES * TILES - STRAIGHT))

    def rows_of(t):
        return pl.ds(pl.multiple_of(t * TILE, TILE), TILE)

    def direct_copy(i, h, t, p):
        return pltpu.make_async_remote_copy(
            src_ref=sb_ref.at[i, h, rows_of(t)], dst_ref=rb_ref.at[h, z, rows_of(t)],
            send_sem=zs_sem.at[i, h, t], recv_sem=zr_sem.at[h, z, t],
            device_id={"feat": p}, device_id_type=MESH_ID)

    def relay_copy(i, h, t, p):
        slot = jnp.where(p > z, 0, 1)
        return pltpu.make_async_remote_copy(
            src_ref=sb_ref.at[i, h, rows_of(t)], dst_ref=relay_ref.at[slot, h, rows_of(t)],
            send_sem=zs_sem.at[i, h, t], recv_sem=yr_sem.at[slot, h, t],
            device_id={"feat": z + p + 2}, device_id_type=MESH_ID)

    def forward_copy(r, h, t):
        low = z // 7
        high = z - 2 - low
        src, dst = (low, high) if r == 0 else (high, low)
        return pltpu.make_async_remote_copy(
            src_ref=relay_ref.at[r, h, rows_of(t)], dst_ref=rb_ref.at[h, src, rows_of(t)],
            send_sem=ys_sem.at[r, h, t], recv_sem=zr_sem.at[h, src, t],
            device_id={"feat": dst}, device_id_type=MESH_ID)

    def seat(j, sign):
        y, x, k = STEPS[j]
        y = lax.rem(c // 8 + (4 + sign * y), 4)
        x = lax.rem(c // 2 % 4 + (4 + sign * x), 4)
        return y * 8 + x * 2 + lax.rem(c + k, 2)

    def unit_copy(h, j):
        q = seat(j, 1)
        return pltpu.make_async_remote_copy(
            src_ref=s2_ref.at[h, q], dst_ref=r2_ref.at[h, j],
            send_sem=us_sem.at[h, j], recv_sem=ur_sem.at[h, j],
            device_id={"clus": q}, device_id_type=MESH_ID)

    def meta_copy(j):
        q = seat(j, 1)
        return pltpu.make_async_remote_copy(
            src_ref=sm_ref.at[q], dst_ref=rm_ref.at[j],
            send_sem=ms_sem.at[j], recv_sem=mr_sem.at[j],
            device_id={"clus": q}, device_id_type=MESH_ID)

    def best_copy(j):
        q = seat(j, -1)
        return pltpu.make_async_remote_copy(
            src_ref=rs_ref.at[j], dst_ref=rr_ref.at[c],
            send_sem=bs_sem.at[j], recv_sem=br_sem.at[c],
            device_id={"clus": q}, device_id_type=MESH_ID)

    def table_copy(p):
        return pltpu.make_async_remote_copy(
            src_ref=tg_ref.at[z], dst_ref=tg_ref.at[z],
            send_sem=ts_sem.at[p], recv_sem=tr_sem.at[z],
            device_id={"feat": p}, device_id_type=MESH_ID)

    def arrival(ref, sem, *index):
        return pltpu.make_async_copy(ref.at[index], ref.at[index], sem.at[index])

    def others(action):
        def one(i, carry):
            action(lax.rem(c + i, PLACES))
            return carry
        lax.fori_loop(1, PLACES, one, 0)

    def chosen(h, p, t):
        keys = key_ref[0:1, h * HALF:(h + 1) * HALF]
        return pick(keys == iota((TILE, HALF), 0) + (p * STRIDE + t * TILE))

    sign = (2 * signs_ref[...] - 1).astype(F32)

    def send_half(h):
        def send_tile(k, carry):
            t = k // (LIVE - 1)
            i = k % (LIVE - 1)
            p = target(i)
            rows = dot(chosen(h, p, t), x_ref[h * HALF:(h + 1) * HALF, :])
            sb_ref[i, h, rows_of(t), :] = (rows * sign).astype(BF)

            @pl.when(far(p, h, t))
            def _():
                relay_copy(i, h, t, p).start()

            @pl.when(jnp.logical_not(far(p, h, t)))
            def _():
                direct_copy(i, h, t, p).start()
            return carry
        lax.fori_loop(0, TILES * (LIVE - 1), send_tile, 0)

    @pl.when(live)
    def _():
        send_half(0)

    over = jnp.maximum(over, rank_half(1))

    @pl.when(live)
    def _():
        send_half(1)

        for h in range(HALVES):
            def own(t, carry, h=h):
                hot = chosen(h, z, t)
                rows = dot(hot, x_ref[h * HALF:(h + 1) * HALF, :])
                rb_ref[h, z, rows_of(t), :] = (rows * sign).astype(BF)
                cm_ref[h, rows_of(t), :] = dot_nt(hot, meta_ref[:, h * HALF:(h + 1) * HALF]).astype(BF)
                return carry
            lax.fori_loop(0, TILES, own, 0)

        def walsh(t, carry):
            at = pl.ds(pl.multiple_of(t * 128, 128), 128)
            both = (iota((128, KEEP), 0) + t * 128) & coords_ref[...]
            both = both ^ (both >> 8)
            both = both ^ (both >> 4)
            both = both ^ (both >> 2)
            both = both ^ (both >> 1)
            had_ref[at, :] = (1 - 2 * (both & 1)).astype(F32).astype(BF)
            return carry
        lax.fori_loop(0, LIVE * WIDTH // 128, walsh, 0)

        unit16 = pick(iota((16, 128), 0) == iota((16, 128), 1))

        def goal_of(h):
            lanes = dot_nt(unit16, cm_ref[h])
            return jnp.where(lanes[4:5] > 0.5, lanes[5:6] * ROOM + lanes[6:7], -1.0).astype(I32)
        goals = [goal_of(h) for h in range(HALVES)]

        def placed(h, g):
            return pick(goals[h] == iota((ROWS, SLOTS), 0) + g * ROWS)

        def send_meta(g, carry):
            for h in range(HALVES):
                info = dot(placed(h, g), cm_ref[h])
                info = jnp.where(iota(info.shape, 1) == 5, over, info)
                sm_ref[pl.ds(g * BATCH, BATCH), h] = info.astype(BF).reshape(BATCH, ROOM, 128)
            return carry
        lax.fori_loop(0, BATCHES, send_meta, 0)

        def keep_own(source, sink):
            own_copy = pltpu.make_async_copy(source, sink, own_sem)
            own_copy.start()
            return own_copy
        kept = keep_own(sm_ref.at[c], rm_ref.at[0])
        for j in range(1, PLACES):
            meta_copy(j).start()
        kept.wait()

        def transform(h):
            def tile(t, carry):
                for s in range(LIVE):
                    @pl.when(z != s)
                    def _():
                        arrived = rb_ref.at[h, s, rows_of(t)]
                        pltpu.make_async_copy(arrived, arrived, zr_sem.at[h, s, t]).wait()
                block = jnp.concatenate([rb_ref[h, s, rows_of(t), :] for s in range(LIVE)], axis=1)
                sketch = dot(block, had_ref[...])
                total = jnp.sum(sketch * sketch, axis=1, keepdims=True)
                unit_ref[h, rows_of(t), :] = (sketch * lax.rsqrt(total + 1e-06)).astype(BF)
                return carry
            lax.fori_loop(0, TILES, tile, 0)

        def send_units(h):
            def one(g, carry):
                rows = dot(placed(h, g), unit_ref[h])
                s2_ref[h, pl.ds(g * BATCH, BATCH)] = rows.astype(BF).reshape(BATCH, ROOM, KEEP)
                return carry
            lax.fori_loop(0, BATCHES, one, 0)
            for j in range(1, PLACES):
                unit_copy(h, j).start()
            keep_own(s2_ref.at[h, c], r2_ref.at[h, 0]).wait()

        before = pick(iota((ROWS, ROWS), 0) < iota((ROWS, ROWS), 1))

        def read_meta(b, carry):
            h = b // BATCHES
            info = rm_ref[pl.ds(lax.rem(b, BATCHES) * BATCH, BATCH), h].reshape(ROWS, 128)
            lanes = dot_nt(unit16, info)
            flag, most = carry
            rank = dot(lanes.astype(BF), before)[4:5]
            flag = jnp.maximum(flag, jnp.max(lanes[5:6]))
            most = jnp.maximum(most, jnp.max(rank + lanes[4:5]))
            position = jnp.where(lanes[4:5] > 0.5, rank, -1.0).astype(I32)
            pos_ref[b] = jnp.broadcast_to(position, (8, ROWS))
            packed = dot(pick(position == iota((FILLED, ROWS), 0)), info)
            key = (packed[:, 0:1] + 256.0 * packed[:, 1:2] + 65536.0 * packed[:, 2:3]).astype(I32)
            key = key + (packed[:, 3:4].astype(I32) << 24)
            key = jnp.where(packed[:, 4:5] > 0.5, key, jnp.int32(2 ** 31 - 1))
            col_ref[b] = jnp.broadcast_to(key, (FILLED, 128))
            lanes = dot_nt(unit16, packed.astype(BF))
            key = (lanes[0:1] + 256.0 * lanes[1:2] + 65536.0 * lanes[2:3]).astype(I32)
            row_ref[b] = jnp.broadcast_to(key + (lanes[3:4].astype(I32) << 24), (8, FILLED))
            return flag, most

        def pack(h, k):
            for j in range(k * BATCH, (k + 1) * BATCH):
                if j:
                    arrival(r2_ref, ur_sem, h, j).wait()
            b = h * BATCHES + k
            rows = r2_ref[h, k * BATCH:(k + 1) * BATCH].reshape(ROWS, KEEP)
            full_ref[b] = dot(pick(pos_ref[b, 0:1] == iota((FILLED, ROWS), 0)), rows).astype(BF)

        def match(i, k):
            mine = row_ref[i, 0:1]
            floor = (mine >> ORDER_BITS) << ORDER_BITS
            key = col_ref[k]
            key = jnp.concatenate([key, key], axis=1)
            score = dot_nt(full_ref[k], full_ref[i])
            score = jnp.where((key < mine) & (key >= floor), score, 0.0)
            return jnp.max(score.reshape(FILLED // 8, 8, FILLED), axis=0)

        def compare(b):
            def queries(k, top):
                return jnp.maximum(top, match(b, k))
            top_ref[b] = lax.fori_loop(0, b + 1, queries, jnp.zeros((8, FILLED), F32), unroll=True)

            def candidates(i, carry):
                top_ref[i] = jnp.maximum(top_ref[i], match(i, b))
                return carry
            lax.fori_loop(0, b, candidates, 0, unroll=True)

        transform(0)
        send_units(0)
        transform(1)
        send_units(1)
        for j in range(1, PLACES):
            arrival(rm_ref, mr_sem, j).wait()
        flag, most = lax.fori_loop(0, BLOCKS, read_meta, (jnp.float32(0), jnp.float32(0)))
        flag = jnp.maximum(flag, jnp.where(most > FILLED, jnp.float32(1), jnp.float32(0)))
        for k in range(BATCHES):
            pack(0, k)
            compare(k)
        for k in range(BATCHES):
            pack(1, k)
            compare(BATCHES + k)
        for b in range(BLOCKS):
            top = jnp.max(top_ref[b], axis=0, keepdims=True)
            high = top.astype(BF).astype(F32)
            middle = (top - high).astype(BF).astype(F32)
            line = iota((16, FILLED), 0)
            parts = jnp.where(line == 0, high, jnp.where(line == 1, middle, jnp.where(line == 2, top - high - middle, 0.0)))
            parts = dot(parts.astype(BF), pick(iota((FILLED, ROWS), 0) == pos_ref[b, 0:1]))
            best_ref[b, :, :ROWS] = jnp.broadcast_to(parts[0:1] + parts[1:2] + parts[2:3], (8, ROWS))
            best_ref[b, :, ROWS:] = jnp.zeros((8, 128), F32)

        for j in range(PLACES):
            start = j % BATCH * ROOM
            left = start // 128 * 128
            pieces = []
            for h in range(HALVES):
                window = best_ref[h * BATCHES + j // BATCH, :, left:left + 256]
                pieces.append(pltpu.roll(window, (256 - (start - left) + h * ROOM) % 256, 1)[:, :128])
            lane = iota((8, 128), 1)
            rs_ref[j] = jnp.where(lane == 127, flag, jnp.where(lane < ROOM, pieces[0], pieces[1]))
            if j:
                best_copy(j).start()
        keep_own(rs_ref.at[0], rr_ref.at[c]).wait()
        others(lambda q: arrival(rr_ref, br_sem, q).wait())
        table = rr_ref[:, 0, :]
        tg_ref[z] = table
        for p in range(8):
            @pl.when(z != p)
            def _():
                table_copy(p).start()

        for h in range(HALVES):
            def sent(k, carry, h=h):
                direct_copy(k % (LIVE - 1), h, k // (LIVE - 1), target(k % (LIVE - 1))).wait_send()
                return carry
            lax.fori_loop(0, TILES * (LIVE - 1), sent, 0)
            for j in range(1, PLACES):
                unit_copy(h, j).wait_send()
        for j in range(1, PLACES):
            meta_copy(j).wait_send()
            best_copy(j).wait_send()
        for p in range(8):
            @pl.when(z != p)
            def _():
                table_copy(p).wait_send()

    @pl.when(jnp.logical_not(live))
    def _():
        def passed(r, h, t, action):
            @pl.when((z == 6) | (h * TILES + t < HALVES * TILES - STRAIGHT))
            def _():
                action(r, h, t)

        def pass_on(r, h, t):
            held = relay_ref.at[r, h, rows_of(t)]
            pltpu.make_async_copy(held, held, yr_sem.at[r, h, t]).wait()
            forward_copy(r, h, t).start()

        for action in (pass_on, lambda r, h, t: forward_copy(r, h, t).wait_send()):
            for h in range(HALVES):
                def tile(t, carry, h=h, action=action):
                    for r in range(2):
                        passed(r, h, t, action)
                    return carry
                lax.fori_loop(0, TILES, tile, 0)

    for p in range(LIVE):
        @pl.when(z != p)
        def _():
            pltpu.make_async_copy(tg_ref.at[p], tg_ref.at[p], tr_sem.at[p]).wait()
    table = tg_ref[...].reshape(DEVS, 128)
    flag_ref[...] = jnp.broadcast_to(jnp.max(jnp.where(iota((DEVS, 128), 1) == 127, table, 0.0)), (1, 128))
    high = table.astype(BF)
    left = table - high.astype(F32)
    middle = left.astype(BF)
    lowest = (left - middle.astype(F32)).astype(BF)
    for t in range(HERE // WIDTH):
        at = pl.ds(pl.multiple_of(z * HERE + t * WIDTH, WIDTH), WIDTH)
        lane = pick(iota((128, WIDTH), 0) == rank_ref[0:1, at])
        found = dot(high, lane) + dot(middle, lane) + dot(lowest, lane)
        found = jnp.where(iota((DEVS, WIDTH), 0) == dev_ref[0:1, at], found, 0.0)
        out_ref[0:1, t * WIDTH:(t + 1) * WIDTH] = jnp.sum(found, axis=0, keepdims=True)


def local(embeddings, signs, coords, cluster, order):
    vmem = pl.BlockSpec(memory_space=pltpu.VMEM)
    dma = pltpu.SemaphoreType.DMA
    best, flag = pl.pallas_call(
        fast_kernel,
        out_shape=(jax.ShapeDtypeStruct((1, HERE), F32), jax.ShapeDtypeStruct((1, 128), F32)),
        in_specs=[pl.BlockSpec(memory_space=pl.ANY)] + [vmem] * 4,
        out_specs=(vmem, vmem),
        scratch_shapes=[
            pltpu.VMEM((1, GROUP), I32),
            pltpu.VMEM((1, GROUP), I32),
            pltpu.VMEM((1, GROUP), I32),
            pltpu.VMEM((128, GROUP), BF),
            pltpu.VMEM((HALVES, SLOTS, 128), BF),
            pltpu.VMEM((LIVE * WIDTH, KEEP), BF),
            pltpu.VMEM((LIVE - 1, HALVES, SLOTS, WIDTH), BF),
            pltpu.VMEM((HALVES, LIVE, SLOTS, WIDTH), BF),
            pltpu.VMEM((2, HALVES, SLOTS, WIDTH), BF),
            pltpu.VMEM((HALVES, SLOTS, KEEP), BF),
            pltpu.VMEM((HALVES, PLACES, ROOM, KEEP), BF),
            pltpu.VMEM((HALVES, PLACES, ROOM, KEEP), BF),
            pltpu.VMEM((PLACES, HALVES, ROOM, 128), BF),
            pltpu.VMEM((PLACES, HALVES, ROOM, 128), BF),
            pltpu.VMEM((BLOCKS, 8, ROWS), I32),
            pltpu.VMEM((BLOCKS, FILLED, KEEP), BF),
            pltpu.VMEM((BLOCKS, FILLED, 128), I32),
            pltpu.VMEM((BLOCKS, 8, FILLED), I32),
            pltpu.VMEM((BLOCKS, 8, FILLED), F32),
            pltpu.VMEM((BLOCKS, 8, ROWS + 128), F32),
            pltpu.VMEM((PLACES, 8, 128), F32),
            pltpu.VMEM((PLACES, 8, 128), F32),
            pltpu.VMEM((LIVE, PLACES, 128), F32),
            dma((LIVE - 1, HALVES, TILES)),
            dma((HALVES, LIVE, TILES)),
            dma((2, HALVES, TILES)),
            dma((2, HALVES, TILES)),
            dma((HALVES, PLACES)),
            dma((HALVES, PLACES)),
            dma((PLACES,)),
            dma((PLACES,)),
            dma((PLACES,)),
            dma((PLACES,)),
            dma((8,)),
            dma((LIVE,)),
            dma,
            pltpu.VMEM((GROUP, WIDTH), BF),
            dma,
        ],
        compiler_params=pltpu.CompilerParams(
            collective_id=0, has_side_effects=True, vmem_limit_bytes=56 * 1024 * 1024
        ),
    )(
        embeddings,
        signs.reshape(1, WIDTH),
        coords.reshape(1, KEEP),
        cluster.reshape(1, GROUP),
        order.reshape(1, GROUP),
    )
    return lax.cond(
        flag[0, 0] > 0.5,
        lambda: general(embeddings, signs, coords, cluster, order),
        lambda: best,
    )


def solution(mesh):
    return jax.shard_map(
        local,
        mesh=mesh,
        in_specs=(P("clus", "feat"), P("feat"), P(), P("clus"), P("clus")),
        out_specs=P("clus", "feat"),
        check_vma=False,
    )
```
